128 devices in a mesh: fsdp: 32 (over x, z, core), dp: 4 (over y).
Axes of the slice: x: 4, y: 4, z: 4, core: 2. Of those that a mesh axis runs over, the one named last changes fastest.
Arguments:
- tokens_in: bfloat16 [2, 32768, 640], P(None, ('fsdp', 'dp')), may hold values from -6 to 6
- cotangent: bfloat16 [2, 32768, 640], P(None, ('fsdp', 'dp')), may hold values from -6 to 6
- doc_lengths: int32 [32, 2, 3], P('fsdp'), may hold values from 1 to 960, 1024 in all within a row
- w_query: bfloat16 [640, 1024], P(('fsdp', 'dp')), may hold values from -0.25 to 0.25
- w_key: bfloat16 [640, 256], P(('fsdp', 'dp')), may hold values from -0.25 to 0.25
- w_value: bfloat16 [640, 256], P(('fsdp', 'dp')), may hold values from -0.25 to 0.25
- w_out: bfloat16 [1024, 640], P(('fsdp', 'dp')), may hold values from -0.1875 to 0.1875
- gain_attn_in: bfloat16 [640], P(('fsdp', 'dp')), may hold values from 0.099609375 to 1.8984375
- gain_attn_out: bfloat16 [640], P(('fsdp', 'dp')), may hold values from 0.099609375 to 1.8984375
- gain_query: bfloat16 [256], P(('fsdp', 'dp')), may hold values from 0.099609375 to 1.8984375
- gain_key: bfloat16 [256], P(('fsdp', 'dp')), may hold values from 0.099609375 to 1.8984375
- w_gate: bfloat16 [640, 2048], P(('fsdp', 'dp')), may hold values from -0.25 to 0.25
- w_up: bfloat16 [640, 2048], P(('fsdp', 'dp')), may hold values from -0.25 to 0.25
- w_down: bfloat16 [2048, 640], P(('fsdp', 'dp')), may hold values from -0.125 to 0.125
- gain_ffn_in: bfloat16 [640], P(('fsdp', 'dp')), may hold values from 0.099609375 to 1.8984375
- gain_ffn_out: bfloat16 [640], P(('fsdp', 'dp')), may hold values from 0.099609375 to 1.8984375
Outputs:
- layer_out: bfloat16 [2, 32768, 640], P(None, ('fsdp', 'dp'))
- grad_tokens: float32 [2, 32768, 640], P(None, ('fsdp', 'dp'))
- grad_query: float32 [640, 1024], P(('fsdp', 'dp'))
- grad_key: float32 [640, 256], P(('fsdp', 'dp'))
- grad_value: float32 [640, 256], P(('fsdp', 'dp'))
- grad_out: float32 [1024, 640], P(('fsdp', 'dp'))
- grad_attn_in: float32 [640], P(('fsdp', 'dp'))
- grad_attn_out: float32 [640], P(('fsdp', 'dp'))
- grad_gain_query: float32 [256], P(('fsdp', 'dp'))
- grad_gain_key: float32 [256], P(('fsdp', 'dp'))
- grad_gate: float32 [640, 2048], P(('fsdp', 'dp'))
- grad_up: float32 [640, 2048], P(('fsdp', 'dp'))
- grad_down: float32 [2048, 640], P(('fsdp', 'dp'))
- grad_ffn_in: float32 [640], P(('fsdp', 'dp'))
- grad_ffn_out: float32 [640], P(('fsdp', 'dp'))
The draws below stay inside these ranges and needn't reach their ends.
Inputs may be any that keep to these rules, and one draw needn't show every extreme that they name: `doc_lengths`: each row of 3 lengths sums to 1024; its largest is exactly 960.
All inputs are finite; a program needn't handle non-finite values.
Results may differ from the reference program's by a relative error of at most 0.035.
Values may be sent and summed in bfloat16 or wider, within the bound.
A program may use at most 192 MiB of HBM per device.

```python
import math
import jax
import jax.numpy as jnp
import numpy as np
from jax import lax

D = 640
FF = 2048
HEADS = 4
HEAD_DIM = 256
MICRO = 2
SEQS = 3
GROUP = 1024
LONGEST = 960
ROWS = 32768
N_FSDP = 32


def block_levels(rng, extent, cuts, smallest, top_value):
    def one(position, parts):
        draws = jax.random.uniform(jax.random.fold_in(jax.random.fold_in(rng, 6), position), (parts,), jnp.float32, smallest / len(cuts), top_value / len(cuts))
        return jnp.repeat(jnp.exp(draws), extent[position] // parts).reshape((-1,) + (1,) * (len(extent) - position - 1))

    gain = one(*cuts[0])
    for cut in cuts[1:]:
        gain = gain * one(*cut)
    return gain


def profile(number_of, total, most, lean):
    portions = [(1 << 20) // math.isqrt(standing ** lean) + 1 for standing in range(2, number_of + 1)]
    surplus, given = total - most - (number_of - 1), [1] * (number_of - 1)
    while surplus > 0:
        candidates = [i for i in range(number_of - 1) if given[i] < most]
        mass, remaining = sum([portions[i] for i in candidates]), surplus
        for i in candidates:
            addition = min(most - given[i], max(1, remaining * portions[i] // mass), surplus)
            given[i] = given[i] + addition
            surplus = surplus - addition
    return np.array([most] + given)


def ragged(key, count, total, reach, skew):
    if count == 2:
        one = jax.random.randint(key, (), max(1, total - reach), min(reach, total - 1) + 1)
        return jnp.stack([one, total - one])
    tallies = jnp.asarray(profile(count, total, reach, skew), jnp.int32)
    twos = (count - 1) // 2
    giver, receiver = tallies[1:1 + 2 * twos:2], tallies[2:2 + 2 * twos:2]
    room = jnp.minimum(giver - 1, reach - receiver)
    shifted = jax.random.randint(jax.random.fold_in(key, 1), (twos,), 0, 1 << 20) % (room + 1)
    tallies = tallies.at[1:1 + 2 * twos:2].set(giver - shifted).at[2:2 + 2 * twos:2].set(receiver + shifted)
    return tallies[jax.random.permutation(jax.random.fold_in(key, 2), count)]


def centred(own_key, shape, spread, reach, split=(), kind=jnp.bfloat16):
    drawn = jax.random.normal(own_key, shape, jnp.float32) * spread
    if len(split) > 0:
        drawn = block_levels(own_key, shape, split, -0.22, 0.18) * drawn
    return jnp.clip(drawn, min=-reach, max=reach).astype(kind)


def setup_inputs(seed: int = 0) -> dict:
    streams_of = jax.random.split(jax.random.key(seed), 17)
    return {
        "tokens_in": centred(streams_of[0], (MICRO, ROWS, D), 1.0, 6.0, ((1, 128),)),
        "cotangent": centred(streams_of[1], (MICRO, ROWS, D), 1.0, 6.0, ((1, 128),)),
        "doc_lengths": jax.vmap(lambda own: ragged(own, SEQS, GROUP, LONGEST, 2))(jax.random.split(streams_of[2], N_FSDP * MICRO)).reshape((N_FSDP, MICRO, SEQS)).astype(jnp.int32),
        "w_query": centred(streams_of[3], (D, HEADS * HEAD_DIM), D ** -0.5, 0.25, ((0, 128),)),
        "w_key": centred(streams_of[4], (D, HEAD_DIM), D ** -0.5, 0.25, ((0, 128),)),
        "w_value": centred(streams_of[5], (D, HEAD_DIM), D ** -0.5, 0.25, ((0, 128),)),
        "w_out": centred(streams_of[6], (HEADS * HEAD_DIM, D), (HEADS * HEAD_DIM) ** -0.5, 0.1875, ((0, 128),)),
        "gain_attn_in": jnp.clip(1.0 + 0.18 * jax.random.normal(streams_of[7], (D,), jnp.float32), 0.099609375, 1.8984375).astype(jnp.bfloat16),
        "gain_attn_out": jnp.clip(1.0 + 0.18 * jax.random.normal(streams_of[8], (D,), jnp.float32), 0.099609375, 1.8984375).astype(jnp.bfloat16),
        "gain_query": jnp.clip(1.0 + 0.18 * jax.random.normal(streams_of[9], (HEAD_DIM,), jnp.float32), 0.099609375, 1.8984375).astype(jnp.bfloat16),
        "gain_key": jnp.clip(1.0 + 0.18 * jax.random.normal(streams_of[10], (HEAD_DIM,), jnp.float32), 0.099609375, 1.8984375).astype(jnp.bfloat16),
        "w_gate": centred(streams_of[11], (D, FF), D ** -0.5, 0.25, ((0, 128),)),
        "w_up": centred(streams_of[12], (D, FF), D ** -0.5, 0.25, ((0, 128),)),
        "w_down": centred(streams_of[13], (FF, D), FF ** -0.5, 0.125, ((0, 128),)),
        "gain_ffn_in": jnp.clip(1.0 + 0.18 * jax.random.normal(streams_of[14], (D,), jnp.float32), 0.099609375, 1.8984375).astype(jnp.bfloat16),
        "gain_ffn_out": jnp.clip(1.0 + 0.18 * jax.random.normal(streams_of[15], (D,), jnp.float32), 0.099609375, 1.8984375).astype(jnp.bfloat16),
    }


@jax.custom_vjp
def low(v):
    return lax.optimization_barrier(v.astype(jnp.bfloat16)).astype(jnp.float32)

@jax.custom_vjp
def low_back(v):
    return v

def low_keep(v):
    return (low(v), None)

def low_pass(kept, grad):
    return (grad,)

def back_keep(v):
    return (v, None)

def back_low(kept, grad):
    return (low(grad),)
low.defvjp(low_keep, low_pass)
low_back.defvjp(back_keep, back_low)
norm_eps = 1e-06
rope_base = 1000000.0
masked_fill = -1e+30

def matmul_high(left, right):
    return jnp.dot(left, right, precision=lax.Precision.HIGHEST, preferred_element_type=jnp.float32)

def rms_scale(value_in, gain_in):
    return value_in * lax.rsqrt(lax.optimization_barrier(jnp.mean(value_in * value_in, -1, keepdims=True)) + norm_eps) * gain_in

def rotate(value_in, cosine, sine_part):
    half_width = value_in.shape[-1] // 2
    first_half = value_in[..., :half_width]
    second_half = value_in[..., half_width:]
    return jnp.concatenate([first_half * cosine - second_half * sine_part, second_half * cosine + first_half * sine_part], -1)

def angles(places, feat_width):
    half_width = feat_width // 2
    inv_freq = jnp.exp(jnp.arange(half_width, dtype=jnp.float32) * (-2.0 * math.log(rope_base) / feat_width))
    turned = places.astype(jnp.float32)[:, None] * inv_freq[None, :]
    return (jnp.cos(turned), jnp.sin(turned))

def doc_layout(lengths, group_rows):
    doc_ends = jnp.cumsum(lengths).astype(jnp.int32)
    order_ids = jnp.arange(group_rows, dtype=jnp.int32)
    passed = (order_ids[:, None] >= doc_ends[None, :]).astype(jnp.int32)
    doc_ids = lax.optimization_barrier(jnp.sum(passed, 1))
    starts = lax.optimization_barrier(jnp.sum(passed * lengths[None, :], 1))
    return (doc_ids, order_ids - starts)

def block(x_group, lengths, params):
    w_query, w_key, w_value, w_out, g_attn_in, g_attn_out, g_query, g_key, w_gate, w_up, w_down, g_ffn_in, g_ffn_out = params
    group_rows = x_group.shape[0]
    doc_ids, places = doc_layout(lengths, group_rows)
    cosine, sine_part = angles(places, HEAD_DIM)
    order_ids = jnp.arange(group_rows, dtype=jnp.int32)
    visible = (doc_ids[:, None] == doc_ids[None, :]) & (order_ids[:, None] >= order_ids[None, :])
    normed = low(rms_scale(x_group, g_attn_in))
    query_raw = low_back(matmul_high(normed, w_query)).reshape(group_rows, HEADS, HEAD_DIM)
    queries = low(rotate(rms_scale(query_raw, g_query), cosine[:, None, :], sine_part[:, None, :]))
    key_raw = low_back(matmul_high(normed, w_key))
    keys_ready = low(rotate(rms_scale(key_raw, g_key), cosine, sine_part))
    values_ready = low(low_back(matmul_high(normed, w_value)))
    scores = low_back(jnp.einsum('thd,sd->hts', queries, keys_ready, precision=lax.Precision.HIGHEST) * HEAD_DIM ** (-0.5))
    scores = jnp.where(visible[None], scores, masked_fill)
    row_max = lax.optimization_barrier(jnp.max(scores, -1, keepdims=True))
    scaled_exp = jnp.exp(scores - row_max)
    attn_probs = low(scaled_exp / lax.optimization_barrier(jnp.sum(scaled_exp, -1, keepdims=True)))
    attn_mix = low(low_back(jnp.einsum('hts,sd->thd', attn_probs, values_ready, precision=lax.Precision.HIGHEST)))
    attn_mix = attn_mix.reshape(group_rows, HEADS * HEAD_DIM)
    branch = low_back(matmul_high(attn_mix, w_out))
    hidden = x_group + rms_scale(branch, g_attn_out)
    normed_ffn = low(rms_scale(hidden, g_ffn_in))
    gate_proj = low_back(matmul_high(normed_ffn, w_gate))
    up_proj = low_back(matmul_high(normed_ffn, w_up))
    hidden_mix = low(jax.nn.gelu(gate_proj, approximate=True) * up_proj)
    down_proj = low_back(matmul_high(hidden_mix, w_down))
    return hidden + rms_scale(down_proj, g_ffn_out)

def reference(tokens_in, cotangent, doc_lengths, w_query, w_key, w_value, w_out, gain_attn_in, gain_attn_out, gain_query, gain_key, w_gate, w_up, w_down, gain_ffn_in, gain_ffn_out):
    lengths = jnp.transpose(doc_lengths, (1, 0, 2)).reshape(-1, doc_lengths.shape[2])
    params = (w_query.astype(jnp.float32), w_key.astype(jnp.float32), w_value.astype(jnp.float32), w_out.astype(jnp.float32), gain_attn_in.astype(jnp.float32), gain_attn_out.astype(jnp.float32), gain_query.astype(jnp.float32), gain_key.astype(jnp.float32), w_gate.astype(jnp.float32), w_up.astype(jnp.float32), w_down.astype(jnp.float32), gain_ffn_in.astype(jnp.float32), gain_ffn_out.astype(jnp.float32))

    def forward(x_all, weights):
        micro_count, rows_all, feat_width = x_all.shape
        group_rows = rows_all // N_FSDP
        grouped = x_all.reshape(micro_count * N_FSDP, group_rows, feat_width)

        def group_step(group_pair):
            return block(group_pair[0], group_pair[1], weights)
        result = lax.map(jax.checkpoint(group_step), (grouped, lengths))
        return result.reshape(micro_count, rows_all, feat_width)
    layer_value, pull_back = jax.vjp(forward, tokens_in.astype(jnp.float32), params)
    grad_x, grad_params = pull_back(cotangent.astype(jnp.float32))
    g_query_w, g_key_w, g_value_w, g_out_w, g_attn_in, g_attn_out, g_query_gain, g_key_gain, g_gate_w, g_up_w, g_down_w, g_ffn_in, g_ffn_out = grad_params
    return (layer_value.astype(jnp.bfloat16), grad_x, g_query_w, g_key_w, g_value_w, g_out_w, g_attn_in, g_attn_out, g_query_gain, g_key_gain, g_gate_w, g_up_w, g_down_w, g_ffn_in, g_ffn_out)
```

```python
import math

import jax
import jax.numpy as jnp
from jax import lax
from jax.experimental import pallas as pl
from jax.experimental.pallas import tpu as pltpu
from jax.sharding import PartitionSpec as P

MESH = pl.DeviceIdType.MESH
F32 = jnp.float32
BF = jnp.bfloat16
I32 = jnp.int32
EPS = 1e-06
THETA = 1000000.0
T = 512
D = 640
GAINS = ((0, 5, 640), (5, 5, 640), (10, 2, 256), (12, 2, 256), (14, 5, 640), (19, 5, 640))
N_SEM = 224


def mm(a, b):
    return lax.dot_general(a, b, (((1,), (0,)), ((), ())), preferred_element_type=F32)


def mm_nt(a, b):
    return lax.dot_general(a, b, (((1,), (1,)), ((), ())), preferred_element_type=F32)


def mm_tn(a, b):
    return lax.dot_general(a, b, (((0,), (0,)), ((), ())), preferred_element_type=F32)


def mean_last(v):
    return jnp.mean(v, -1, keepdims=True)


def inv_rms(v):
    return lax.rsqrt(mean_last(v * v) + EPS)


def iota(shape, dim):
    return lax.broadcasted_iota(I32, shape, dim)


def norm_back(v, gain, grad):
    r = inv_rms(v)
    hat = v * r
    gg = grad * gain
    return r * (gg - hat * mean_last(gg * hat)), grad * hat


def kernel(
    tok, cot, dl, gains, wq, wk, wv, wo, wg, wu, wd,
    o_layer, o_gx, o_q, o_k, o_v, o_o, o_gate, o_up, o_down, o_g0, o_g1, o_g2, o_g3, o_g4, o_g5,
    W1, W2, W3, W4, W5, GW, stf, stage, R1, mf, po, PR, DLB,
    XB, CB, NRM, CS, SN, DCOL, DROW, GV, QR, Q, KR, KV, AM, LI, OA, LA, BR, HID, NF, GT, UT, HM, ACC, GD, LO,
    DAM, DD, DKV, DKR, GXR,
    G2, G3, G4, G5, C1, C2, C3, C4, C5, A1, A2, A3, A4, A5, B1, B2, B3, B4, B5, E1, E2, E3, E4, E5,
    GG, GGR, F2, R2, c4f, R4, ss, rs, ls,
):
    f = lax.axis_index("fsdp")
    y = lax.axis_index("dp")
    x = f // 8
    z = (f // 2) % 4
    c = f % 2
    zh, zl = z // 2, z % 2
    me = {"x": x, "z": z, "c": c, "y": y}
    gi = c * 8 + zl * 4 + y
    ge = zl * 8 + c * 4 + y

    def dev(co):
        return ((co["x"] * 4 + co["z"]) * 2 + co["c"], co["y"])

    def member(j):
        return {"x": x, "z": zh * 2 + (j // 4) % 2, "c": j // 8, "y": j % 4}

    def moved(axis, k):
        co = dict(me)
        co[axis] = (me[axis] + k) % (2 if axis == "c" else 4)
        return co

    count = [0]

    def fresh():
        count[0] += 1
        assert count[0] <= N_SEM
        return count[0] - 1

    sent = []

    def send(src, dst, co):
        i = fresh()
        cp = pltpu.make_async_remote_copy(
            src_ref=src, dst_ref=dst, send_sem=ss.at[i], recv_sem=rs.at[i], device_id=dev(co), device_id_type=MESH
        )
        cp.start()
        sent.append(cp)
        return cp

    def arrived(cps):
        for cp in cps:
            cp.wait_recv()

    def sl_cols(r0, rn):
        def sl(co, done):
            xs = slice(None) if "x" in done else pl.ds(co["x"], 1)
            zs = slice(None) if "z" in done else pl.ds(co["z"] // 2, 1)
            if "y" not in done:
                cs, w = co["c"] * 1024 + (co["z"] % 2) * 512 + co["y"] * 128, 128
            elif "z" not in done:
                cs, w = co["c"] * 1024 + (co["z"] % 2) * 512, 512
            else:
                cs, w = co["c"] * 1024, 1024
            return (xs, zs, pl.ds(r0, rn), pl.ds(pl.multiple_of(cs, 128), w))
        return sl

    def sl_out(co, done):
        xs = slice(None) if "x" in done else pl.ds(co["x"], 1)
        zs = slice(None) if "z" in done else pl.ds(co["z"], 1)
        if "y" in done:
            return (xs, zs, pl.ds(co["c"], 1), pl.ds(0, 32), pl.ds(0, 768))
        return (
            xs, zs, pl.ds(co["c"], 1),
            pl.ds(pl.multiple_of((co["y"] // 2) * 16, 16), 16), pl.ds(pl.multiple_of((co["y"] % 2) * 384, 128), 384),
        )

    def sl_down(co, done):
        xs = slice(None) if "x" in done else pl.ds(co["x"], 1)
        zs = slice(None) if "z" in done else pl.ds(co["z"], 1)
        rows = pl.ds(0, 64) if "y" in done else pl.ds(pl.multiple_of(co["y"] * 16, 16), 16)
        return (xs, zs, pl.ds(co["c"], 1), rows, pl.ds(0, 640))

    pieces = {
        "1a": (W1, sl_cols(0, 48), "yzx"),
        "1b": (W1, sl_cols(48, 32), "yxz"),
        "2": (W2, sl_cols(0, 80), "yzx"),
        "3": (W3, sl_cols(0, 80), "yxz"),
        "4": (W4, sl_out, "yzx"),
        "5": (W5, sl_down, "zxy"),
    }

    def gather(name, phase):
        w, sl, order = pieces[name]
        ref = w.at[sl(me, order[:phase])]
        if phase == 3:
            return [send(ref, ref, moved("c", 1))]
        return [send(ref, ref, moved(order[phase], k)) for k in (1, 2, 3)]

    bar = pltpu.get_barrier_semaphore()
    friends = [member((gi + d) % 16) for d in range(1, 16)]
    friends += [moved("z", 2)] + [dict(me, z=(zh * 2 + 2) % 4 + (1 - zl))] + [moved("x", k) for k in (1, 2, 3)]
    for co in friends:
        pl.semaphore_signal(bar, inc=1, device_id=dev(co), device_id_type=MESH)

    grow = gains[...].astype(F32)
    for j in range(16):
        cols = slice(128 * j, 128 * j + 128)
        if j < 8:
            part = wq[:, cols]
        elif j < 10:
            part = wk[:, 128 * (j - 8):128 * (j - 7)]
        elif j < 12:
            part = wv[:, 128 * (j - 10):128 * (j - 9)]
        else:
            part = None
        stf[j, 0:5, :] = jnp.zeros((5, 128), F32) if part is None else part.astype(F32)
        stf[j, 5:10, :] = wg[:, cols].astype(F32)
        stf[j, 10:15, :] = wu[:, cols].astype(F32)
        stf[j, 15:16, :] = grow
    stage[...] = stf[...].astype(BF)
    wof = wo[...].astype(F32)
    twice = jnp.concatenate([wof, wof], axis=0)
    keep = (iota((16, 640), 0) // 8) == (y % 2)
    twice = jnp.where(keep, twice, 0.0).astype(BF)
    po[0, :, :] = twice[:, 0:384]
    po[1, :, 0:256] = twice[:, 384:640]
    po[1, :, 256:384] = jnp.zeros((16, 128), BF)
    rowid = iota((8, 128), 0)
    tile = jnp.zeros((8, 128), I32)
    for m in range(2):
        for k in range(3):
            tile = jnp.where(rowid == 3 * m + k, dl[0, m, k], tile)
    DLB[c] = tile
    W5[x, z, c, pl.ds(pl.multiple_of(y * 16, 16), 16), :] = wd[...]

    pl.semaphore_wait(bar, len(friends))

    core_to = ((y + 1) // 2) % 2
    blocks = (c, 3 - c)

    def reshard(src, dst):
        s_base, r_base = fresh(), fresh()
        s2, r2 = fresh(), fresh()
        ops = []
        for m, si in ((0, s_base), (1, s2)):
            to = dict(me, c=core_to, y=c + 2 * m)
            own = jnp.logical_and(to["c"] == c, to["y"] == y)
            slot = y // 2

            def far(r, m=m, si=si, to=to):
                return pltpu.make_async_remote_copy(
                    src_ref=src.at[m], dst_ref=dst.at[0 if r == r_base else 1], send_sem=ss.at[si],
                    recv_sem=rs.at[r], device_id=dev(to), device_id_type=MESH,
                )

            for sv, r in ((0, r_base), (1, r2)):
                @pl.when(jnp.logical_and(jnp.logical_not(own), slot == sv))
                def _(far=far, r=r):
                    far(r).start()

                @pl.when(jnp.logical_and(own, slot == sv))
                def _(m=m, sv=sv):
                    cp = pltpu.make_async_copy(src.at[m], dst.at[sv], ls)
                    cp.start()
                    cp.wait()

            ops.append((own, far(r_base)))

        def wait_in():
            for s, r in ((0, r_base), (1, r2)):
                mine = jnp.logical_and(blocks[s] == y, c == y % 2)

                @pl.when(jnp.logical_not(mine))
                def _(s=s, r=r):
                    pltpu.make_async_remote_copy(
                        src_ref=src.at[0], dst_ref=dst.at[s], send_sem=ss.at[s_base], recv_sem=rs.at[r],
                        device_id=dev(moved("c", 1)), device_id_type=MESH,
                    ).wait_recv()

        def wait_out():
            for own, cp in ops:
                @pl.when(jnp.logical_not(own))
                def _(cp=cp):
                    cp.wait_send()

        return wait_in, wait_out

    def unshard(src, dst):
        r0, r1 = fresh(), fresh()
        ops = []
        m = y // 2
        for s, si in ((0, r0), (1, r1)):
            to = dict(me, c=y % 2, y=blocks[s])
            own = jnp.logical_and(to["c"] == c, to["y"] == y)

            def far(mv, r, s=s, si=si, to=to):
                return pltpu.make_async_remote_copy(
                    src_ref=src.at[s], dst_ref=dst.at[mv], send_sem=ss.at[si], recv_sem=rs.at[r],
                    device_id=dev(to), device_id_type=MESH,
                )

            for mv, r in ((0, r0), (1, r1)):
                @pl.when(jnp.logical_and(jnp.logical_not(own), m == mv))
                def _(far=far, mv=mv, r=r):
                    far(mv, r).start()

                @pl.when(jnp.logical_and(own, m == mv))
                def _(s=s, mv=mv):
                    cp = pltpu.make_async_copy(src.at[s], dst.at[mv], ls)
                    cp.start()
                    cp.wait()

            ops.append((own, far(0, r0)))

        def wait_in():
            for mv, r in ((0, r0), (1, r1)):
                mine = jnp.logical_and(core_to == c, y == c + 2 * mv)

                @pl.when(jnp.logical_not(mine))
                def _(mv=mv, r=r):
                    pltpu.make_async_remote_copy(
                        src_ref=src.at[0], dst_ref=dst.at[mv], send_sem=ss.at[r0], recv_sem=rs.at[r],
                        device_id=dev(moved("c", 1)), device_id_type=MESH,
                    ).wait_recv()

        def wait_out():
            for own, cp in ops:
                @pl.when(jnp.logical_not(own))
                def _(cp=cp):
                    cp.wait_send()

        return wait_in, wait_out

    a2a = []
    for d in range(1, 16):
        j = (gi + d) % 16
        a2a.append(send(stage.at[j], R1.at[ge], member(j)))
    R1[ge] = stage[gi]
    pair = [send(po.at[1 - y % 2], PR, dict(me, y=y + 1 - 2 * (y % 2)))]
    lens_cp = [send(DLB.at[c], DLB.at[c], moved("c", 1))]
    x_in, x_out = reshard(tok, XB)

    arrived(a2a)
    for e in range(16):
        v = R1[e].astype(F32)
        for k in range(3):
            mf[k, 5 * e:5 * e + 5, :] = v[5 * k:5 * k + 5, :]
        mf[3, e:e + 1, :] = v[15:16, :]
    own_cols = pl.ds(pl.multiple_of(c * 1024 + zl * 512 + y * 128, 128), 128)
    for w, k in ((W1, 0), (W2, 1), (W3, 2)):
        w[x, zh, :, own_cols] = mf[k].astype(BF)
    GW[x, zh] = mf[3, 0:16, :].astype(BF)
    g1a, g1b = gather("1a", 0), gather("1b", 0)
    gz = [send(GW.at[x, zh], GW.at[x, zh], moved("z", 2))]
    arrived(pair)
    W4[x, z, c, pl.ds(pl.multiple_of((y // 2) * 16, 16), 16), pl.ds(pl.multiple_of((y % 2) * 384, 128), 384)] = (
        po[y % 2].astype(F32) + PR[...].astype(F32)
    ).astype(BF)

    arrived(lens_cp)
    lt = DLB[y % 2]
    first = y // 2 == 0
    l0 = jnp.where(first, lt[0:1, :], lt[3:4, :])[:, 0:1]
    l1 = jnp.where(first, lt[1:2, :], lt[4:5, :])[:, 0:1]
    e0, e1 = l0, l0 + l1
    freq = jnp.exp(iota((1, 128), 1).astype(F32) * (-2.0 * math.log(THETA) / 256))
    for s in range(2):
        t = blocks[s] * 256 + iota((256, 1), 0)
        p0, p1 = (t >= e0).astype(I32), (t >= e1).astype(I32)
        DCOL[s] = p0 + p1
        turned = (t - p0 * l0 - p1 * l1).astype(F32) * freq
        CS[s] = jnp.cos(turned)
        SN[s] = jnp.sin(turned)
    for k in range(4):
        t = 256 * k + iota((1, 256), 1)
        DROW[k] = (t >= e0).astype(I32) + (t >= e1).astype(I32)

    arrived(g1a + g1b)
    g1a, g1b = gather("1a", 1), gather("1b", 1)
    arrived(gz)
    gx = [send(GW.at[x], GW.at[x], moved("x", k)) for k in (1, 2, 3)]
    g2, g3, g4, g5 = gather("2", 0), gather("3", 0), gather("4", 0), gather("5", 0)
    x_in()
    arrived(g1a + g1b)
    g1a, g1b = gather("1a", 2), gather("1b", 2)
    arrived(gx)

    packed = GW[...].reshape(128, 128)
    for k, (lane, per, width) in enumerate(GAINS):
        col = iota((128, width), 1)
        shard = iota((128, width), 0)
        colf = col.astype(F32)
        rest = colf - per * jnp.floor((colf + 0.5) * (1.0 / per))
        pick = jnp.where(shard.astype(F32) == rest + lane, 1.0, 0.0).astype(BF)
        spread = mm(packed, pick)
        mine = jnp.logical_and(col >= per * shard, col < per * shard + per)
        GV[k:k + 1, 0:width] = jnp.sum(jnp.where(mine, spread, 0.0), 0, keepdims=True)

    def rows(n, fn):
        def step(i, carry):
            fn(pl.ds(pl.multiple_of(i * n, n), n))
            return carry
        lax.fori_loop(0, T // n, step, 0)

    xv = XB.reshape(T, D)
    cv = CB.reshape(T, D)
    csv, snv = CS.reshape(T, 128), SN.reshape(T, 128)

    def do_norm(r):
        v = xv[r, :].astype(F32)
        NRM[r, :] = (v * inv_rms(v) * GV[0:1, :]).astype(BF)
    rows(128, do_norm)
    arrived(g1a + g1b)
    g1a, g1b = gather("1a", 3), gather("1b", 3)
    arrived(g2 + g3 + g4 + g5)
    g4, g2, g3, g5 = gather("4", 1), gather("2", 1), gather("3", 1), gather("5", 1)
    arrived(g1a + g1b)

    def w1_cols(start, width):
        return W1[:, :, :, pl.ds(pl.multiple_of(start, 128), width)].reshape(D, width)

    def turn(u, cs, sn):
        u1, u2 = u[:, 0:128], u[:, 128:256]
        return u1 * cs - u2 * sn, u2 * cs + u1 * sn

    def turn_back(u, cs, sn):
        u1, u2 = u[:, 0:128], u[:, 128:256]
        return jnp.concatenate([u1 * cs + u2 * sn, u2 * cs - u1 * sn], -1)

    raw = mm(NRM[...], w1_cols(1024, 256))
    KR[...] = raw
    o1, o2 = turn(raw * inv_rms(raw) * GV[3:4, 0:256], csv[...], snv[...])
    vals = mm(NRM[...], w1_cols(1280, 256))
    for s in range(2):
        r = slice(256 * s, 256 * s + 256)
        KV[blocks[s], :, 0:128] = o1[r].astype(BF)
        KV[blocks[s], :, 128:256] = o2[r].astype(BF)
        KV[blocks[s], :, 256:512] = vals[r].astype(BF)
    kv_cp = [send(KV.at[blocks[s]], KV.at[blocks[s]], moved("c", 1)) for s in range(2)]

    def do_query(h, carry):
        raw = mm(NRM[...], w1_cols(h * 256, 256))
        QR[h] = raw.astype(BF)
        o1, o2 = turn(raw * inv_rms(raw) * GV[2:3, 0:256], csv[...], snv[...])
        for s in range(2):
            r = slice(256 * s, 256 * s + 256)
            Q[s, h, :, 0:128] = (o1[r] * 0.0625).astype(BF)
            Q[s, h, :, 128:256] = (o2[r] * 0.0625).astype(BF)
        return carry
    lax.fori_loop(0, 4, do_query, 0)

    arrived(g2 + g3 + g4 + g5)
    g4, g2, g3, g5 = gather("4", 2), gather("2", 2), gather("3", 2), gather("5", 2)
    c_in, c_out = reshard(cot, CB)
    arrived(kv_cp)

    def seen(s, kb):
        t = blocks[s] * 256 + iota((256, 256), 0)
        k = kb * 256 + iota((256, 256), 1)
        return jnp.logical_and(DCOL[s] == DROW[kb], t >= k)

    for s in range(2):
        OA[...] = jnp.zeros_like(OA)
        LA[...] = jnp.zeros_like(LA)

        def forward(kb, carry, s=s):
            vis = seen(s, kb)
            keys, vals = KV[kb, :, 0:256], KV[kb, :, 256:512]
            for h in range(4):
                p = jnp.where(vis, jnp.exp(mm_nt(Q[s, h], keys)), 0.0)
                LA[h] += jnp.sum(p, -1, keepdims=True)
                OA[h] += mm(p.astype(BF), vals)
            return carry
        lax.fori_loop(0, blocks[s] + 1, forward, 0)
        for h in range(4):
            inv = 1.0 / LA[h]
            LI[s, h] = inv
            AM[256 * s:256 * s + 256, 256 * h:256 * h + 256] = (OA[h] * inv).astype(BF)
        if s == 0:
            arrived(g4)
            g4 = gather("4", 3)
    arrived(g4)
    w4v = W4.reshape(1024, 768)
    w5v = W5.reshape(2048, 640)

    def do_out(r):
        b = mm(AM[r, :], w4v[:, 0:640])
        BR[r, :] = b
        hid = xv[r, :].astype(F32) + b * inv_rms(b) * GV[1:2, :]
        HID[r, :] = hid
        NF[r, :] = (hid * inv_rms(hid) * GV[4:5, :]).astype(BF)
    rows(256, do_out)
    arrived(g2 + g3 + g5)
    g2, g3, g5 = gather("2", 3), gather("3", 3), gather("5", 3)
    arrived(g2 + g3 + g5)

    def cols_of(w, at, width):
        return w[:, :, :, pl.ds(pl.multiple_of(at, 128), width)].reshape(D, width)

    def do_ffn(n, carry):
        at = pl.ds(pl.multiple_of(n * 256, 256), 256)
        gate = mm(NF[...], cols_of(W2, n * 256, 256))
        up = mm(NF[...], cols_of(W3, n * 256, 256))
        GT[:, at] = gate.astype(BF)
        UT[:, at] = up.astype(BF)
        HM[:, at] = (jax.nn.gelu(gate, approximate=True) * up).astype(BF)
        return carry
    lax.fori_loop(0, 8, do_ffn, 0)

    c_in()
    GG[...] = jnp.zeros_like(GG)
    lov = LO.reshape(T, D)

    def do_down(r):
        d = mm(HM[r, :], w5v[...])
        rd = inv_rms(d)
        hat = d * rd
        lov[r, :] = (HID[r, :] + hat * GV[5:6, :]).astype(BF)
        g = cv[r, :].astype(F32)
        gg = g * GV[5:6, :]
        GD[r, :] = (rd * (gg - hat * mean_last(gg * hat))).astype(BF)
        GG[5:6, :] += jnp.sum(g * hat, 0, keepdims=True)
    rows(256, do_down)
    lo_in, lo_out = unshard(LO, o_layer)

    g5v = G5.reshape(2048, 640)
    ACC[...] = jnp.zeros_like(ACC)

    def do_ffn_back(n, carry):
        at = pl.ds(pl.multiple_of(n * 256, 256), 256)
        g5v[at, :] = mm_tn(HM[:, at], GD[...]).astype(BF)
        dh = mm_nt(GD[...], w5v[at, :])
        gate, up = GT[:, at].astype(F32), UT[:, at].astype(F32)
        k0, k1 = math.sqrt(2.0 / math.pi), 0.044715
        th = jnp.tanh(k0 * (gate + k1 * gate * gate * gate))
        half = 0.5 * (1.0 + th)
        slope = half + 0.5 * gate * (1.0 - th * th) * k0 * (1.0 + 3.0 * k1 * gate * gate)
        dg = (dh * up * slope).astype(BF)
        du = (dh * (gate * half)).astype(BF)
        nf = NF[...]
        G2[:, :, :, at] = mm_tn(nf, dg).astype(BF).reshape(4, 2, 80, 256)
        G3[:, :, :, at] = mm_tn(nf, du).astype(BF).reshape(4, 2, 80, 256)
        ACC[...] += mm_nt(dg, cols_of(W2, n * 256, 256)) + mm_nt(du, cols_of(W3, n * 256, 256))
        return carry
    lax.fori_loop(0, 8, do_ffn_back, 0)

    red = {
        "2": (G2, sl_cols(0, 80), "yzx", C2, (A2, B2, E2)),
        "3": (G3, sl_cols(0, 80), "yxz", C3, (A3, B3, E3)),
        "4": (G4, sl_out, "yzx", C4, (A4, B4, E4)),
        "5": (G5, sl_down, "zxy", C5, (A5, B5, E5)),
        "1": (W2, sl_cols(0, 80), "yzx", C1, (A1, B1, E1)),
    }

    def sum_core(name):
        g, sl, order, cbuf, _ = red[name]
        return [send(g.at[sl(moved("c", 1), order)], cbuf, moved("c", 1))]

    def leading(shape):
        return shape[0] * shape[1]

    def part(ref_idx, i, shape):
        n1 = shape[1]
        def one(s, k):
            base = 0 if s == slice(None) else s.start
            return pl.ds(base + k, 1)
        return (one(ref_idx[0], i // n1), one(ref_idx[1], i % n1)) + tuple(ref_idx[2:])

    def add_in(name, idx, bufs, out=None):
        g = red[name][0]
        shape = bufs[0].shape

        def step(i, carry):
            at = part(idx, i, shape)
            bat = (pl.ds(i // shape[1], 1), pl.ds(i % shape[1], 1))
            tot = g[at].astype(F32)
            for b in bufs:
                tot = tot + b[bat].astype(F32)
            if out is None:
                g[at] = tot.astype(BF)
            else:
                out(tot)
            return carry
        if leading(shape) == 1:
            step(0, 0)
        else:
            lax.fori_loop(0, leading(shape), step, 0)

    def add_core(name, cps):
        arrived(cps)
        g, sl, order, cbuf, _ = red[name]
        add_in(name, sl(me, order), [cbuf])

    def sum_phase(name, phase):
        g, sl, order, _, bufs = red[name]
        axis, done = order[2 - phase], order[:2 - phase]
        out = []
        for k in (1, 2, 3):
            co = moved(axis, k)
            out.append(send(g.at[sl(co, done)], bufs[phase].at[k - 1], co))
        return out

    def add_phase(name, phase, cps, out=None):
        arrived(cps)
        g, sl, order, _, bufs = red[name]
        add_in(name, sl(me, order[:2 - phase]), [bufs[phase].at[k] for k in range(3)], out)

    s2, s3, s5 = sum_core("2"), sum_core("3"), sum_core("5")

    def do_mid(r):
        g = cv[r, :].astype(F32)
        dv, rowg = norm_back(HID[r, :], GV[4:5, :], ACC[r, :])
        GG[4:5, :] += jnp.sum(rowg, 0, keepdims=True)
        gh = g + dv
        HID[r, :] = gh
        db, rowo = norm_back(BR[r, :], GV[1:2, :], gh)
        GG[1:2, :] += jnp.sum(rowo, 0, keepdims=True)
        GD[r, :] = db.astype(BF)
    rows(128, do_mid)
    g4v = G4.reshape(1024, 768)

    def do_out_grad(n, carry):
        at = pl.ds(pl.multiple_of(n * 256, 256), 256)
        am = AM[:, at]
        g4v[at, 0:640] = mm_tn(am, GD[...]).astype(BF)
        g4v[at, 640:768] = jnp.zeros((256, 128), BF)
        dam = mm_nt(GD[...], w4v[at, 0:640]).astype(BF)
        inner = jnp.sum(dam.astype(F32) * am.astype(F32), -1, keepdims=True)
        for s in range(2):
            DAM[s, n] = dam[256 * s:256 * s + 256]
            DD[s, n] = inner[256 * s:256 * s + 256]
        return carry
    lax.fori_loop(0, 4, do_out_grad, 0)
    add_core("2", s2)
    s2 = sum_phase("2", 0)
    add_core("3", s3)
    s3 = sum_phase("3", 0)
    add_core("5", s5)
    s5 = sum_phase("5", 0)
    s4 = sum_core("4")

    DKV[...] = jnp.zeros_like(DKV)
    for s in range(2):
        OA[...] = jnp.zeros_like(OA)

        def backward(kb, carry, s=s):
            vis = seen(s, kb)
            keys, vals = KV[kb, :, 0:256], KV[kb, :, 256:512]
            dk = jnp.zeros((256, 256), F32)
            dv = jnp.zeros((256, 256), F32)
            for h in range(4):
                q, da = Q[s, h], DAM[s, h]
                p = jnp.where(vis, jnp.exp(mm_nt(q, keys)) * LI[s, h], 0.0)
                ds = (p * (mm_nt(da, vals) - DD[s, h])).astype(BF)
                OA[h] += mm(ds, keys)
                dk = dk + mm_tn(ds, q)
                dv = dv + mm_tn(p.astype(BF), da)
            DKV[kb, :, 0:256] += dk
            DKV[kb, :, 256:512] += dv
            return carry
        lax.fori_loop(0, blocks[s] + 1, backward, 0)

        def query_back(h, carry, s=s):
            dq = turn_back(OA[h] * 0.0625, CS[s], SN[s])
            raw = QR[h, 256 * s:256 * s + 256, :].astype(F32)
            dv, rowg = norm_back(raw, GV[2:3, 0:256], dq)
            GG[2:3, 0:256] += jnp.sum(rowg, 0, keepdims=True)
            GT[256 * s:256 * s + 256, pl.ds(pl.multiple_of(h * 256, 256), 256)] = dv.astype(BF)
            return carry
        lax.fori_loop(0, 4, query_back, 0)
        if s == 0:
            add_core("4", s4)
            s4 = sum_phase("4", 0)
    for s in range(2):
        HM[256 * s:256 * s + 256, 0:512] = DKV[1 - c if s == 0 else 2 + c].astype(BF)
    dk_cp = [send(HM.at[:, pl.ds(0, 512)], DKR, moved("c", 1))]
    for cp in sent:
        cp.wait_send()
    sent.clear()
    add_phase("2", 0, s2)
    s2 = sum_phase("2", 1)
    add_phase("3", 0, s3)
    s3 = sum_phase("3", 1)
    add_phase("5", 0, s5)
    s5 = sum_phase("5", 1)
    add_phase("4", 0, s4)
    s4 = sum_phase("4", 1)
    arrived(dk_cp)
    for s in range(2):
        r = slice(256 * s, 256 * s + 256)
        tot = DKV[blocks[s]] + DKR[r, :].astype(F32)
        dk = turn_back(tot[:, 0:256], CS[s], SN[s])
        dv, rowg = norm_back(KR[r, :], GV[3:4, 0:256], dk)
        GG[3:4, 0:256] += jnp.sum(rowg, 0, keepdims=True)
        GT[r, 1024:1280] = dv.astype(BF)
        GT[r, 1280:1536] = tot[:, 256:512].astype(BF)

    nrm = NRM

    def do_qkv_grad(n, carry):
        at = pl.ds(pl.multiple_of(n * 256, 256), 256)
        W2[:, :, :, at] = mm_tn(nrm[...], GT[:, at]).astype(BF).reshape(4, 2, 80, 256)
        return carry
    lax.fori_loop(0, 6, do_qkv_grad, 0)
    W2[:, :, :, 1536:2048] = jnp.zeros((4, 2, 80, 512), BF)
    s1 = sum_core("1")
    ACC[...] = jnp.zeros_like(ACC)

    def do_dnorm(n, carry):
        at = pl.ds(pl.multiple_of(n * 256, 256), 256)
        ACC[...] += mm_nt(GT[:, at], w1_cols(n * 256, 256))
        return carry
    lax.fori_loop(0, 6, do_dnorm, 0)
    lo_out()
    gxv = LO.reshape(T, D)

    def do_x(r):
        dv, rowg = norm_back(xv[r, :].astype(F32), GV[0:1, :], ACC[r, :])
        GG[0:1, :] += jnp.sum(rowg, 0, keepdims=True)
        gxv[r, :] = (HID[r, :] + dv).astype(BF)
    rows(128, do_x)
    gx_in, gx_out = unshard(LO, GXR)
    add_core("1", s1)
    s1 = sum_phase("1", 0)

    gcp = [send(GG, GGR.at[0], moved("c", 1))]
    add_phase("2", 1, s2)
    s2 = sum_phase("2", 2)
    add_phase("3", 1, s3)
    s3 = sum_phase("3", 2)
    add_phase("5", 1, s5)
    s5 = sum_phase("5", 2)
    add_phase("4", 1, s4)
    s4 = sum_phase("4", 2)
    arrived(gcp)
    base = 1
    tot = GG[...] + GGR[0]
    gcps = []
    for a, axis in enumerate("zyx"):
        GGR[10 + a] = tot
        gcps = [send(GGR.at[10 + a], GGR.at[base + k - 1], moved(axis, k)) for k in (1, 2, 3)]
        arrived(gcps)
        for k in range(3):
            tot = tot + GGR[base + k]
        base += 3
        if a == 0:
            add_phase("1", 0, s1)
            s1 = sum_phase("1", 1)
        if a == 1:
            add_phase("1", 1, s1)
            s1 = sum_phase("1", 2)
    shard = f * 4 + y
    for ref, (k, (lane, per, width)) in zip((o_g0, o_g1, o_g2, o_g3, o_g4, o_g5), enumerate(GAINS)):
        line = tot[k:k + 1, 0:width]
        col = iota((1, width), 1)
        for r in range(per):
            ref[0:1, r:r + 1] = jnp.sum(jnp.where(col == per * shard + r, line, 0.0), 1, keepdims=True)

    def into(k):
        def out(v):
            mf[k] = v.reshape(80, 128)
        return out

    def out_down(v):
        o_down[...] = v.reshape(16, 640)

    def out_4(v):
        c4f[...] = v.reshape(16, 384)

    add_phase("2", 2, s2, into(1))
    add_phase("3", 2, s3, into(2))
    add_phase("5", 2, s5, out_down)
    add_phase("4", 2, s4, out_4)
    pair = [send(c4f.at[pl.ds(pl.multiple_of(8 * (1 - y % 2), 8), 8), :], R4, dict(me, y=y + 1 - 2 * (y % 2)))]
    add_phase("1", 2, s1, into(0))
    for e in range(16):
        for k in range(3):
            F2[e, 5 * k:5 * k + 5, :] = mf[k, 5 * e:5 * e + 5, :]
    home = []
    for d in range(1, 16):
        j = (gi + d) % 16
        home.append(send(F2.at[(j // 4) % 2 * 8 + j // 8 * 4 + j % 4], R2.at[gi], member(j)))
    R2[gi] = F2[ge]
    arrived(pair)
    own = c4f[pl.ds(pl.multiple_of(8 * (y % 2), 8), 8), :]
    left = y % 2 == 0
    o_o[:, 0:384] = jnp.where(left, own, R4[...])
    o_o[:, 384:640] = jnp.where(left, R4[...], own)[:, 0:256]
    gx_in()
    for m in range(2):
        o_gx[m] = GXR[m].astype(F32)
    arrived(home)
    for j in range(16):
        cols = slice(128 * j, 128 * j + 128)
        v = R2[j]
        if j < 8:
            o_q[:, cols] = v[0:5]
        elif j < 10:
            o_k[:, 128 * (j - 8):128 * (j - 7)] = v[0:5]
        elif j < 12:
            o_v[:, 128 * (j - 10):128 * (j - 9)] = v[0:5]
        o_gate[:, cols] = v[5:10]
        o_up[:, cols] = v[10:15]
    lo_in()
    for w in (x_out, c_out, gx_out):
        w()
    for cp in sent:
        cp.wait_send()


def scratch():
    def v(*shape, dtype=F32):
        return pltpu.VMEM(shape, dtype)

    def b(*shape):
        return pltpu.VMEM(shape, BF)

    cols = (4, 2, 80, 2048)
    out = [
        b(*cols), b(*cols), b(*cols), b(4, 4, 2, 32, 768), b(4, 4, 2, 64, 640), b(4, 2, 16, 128),
        v(16, 16, 128), b(16, 16, 128), b(16, 16, 128), v(4, 80, 128), b(2, 16, 384), b(16, 384),
        v(2, 8, 128, dtype=I32),
        b(2, 256, D), b(2, 256, D), b(T, D), v(2, 256, 128), v(2, 256, 128),
        v(2, 256, 1, dtype=I32), v(4, 1, 256, dtype=I32), v(8, D),
        b(4, T, 256), b(2, 4, 256, 256), v(T, 256), b(4, 256, 512), b(T, 1024),
        v(2, 4, 256, 1), v(4, 256, 256), v(4, 256, 1),
        v(T, D), v(T, D), b(T, D), b(T, 2048), b(T, 2048), b(T, 2048), v(T, D), b(T, D),
        b(2, 256, D),
        b(2, 4, 256, 256), v(2, 4, 256, 1), v(4, 256, 512), b(T, 512),
        b(2, 256, D),
        b(*cols), b(*cols), b(4, 4, 2, 32, 768), b(4, 4, 2, 64, 640),
        b(4, 2, 80, 1024), b(4, 2, 80, 1024), b(4, 2, 80, 1024), b(4, 4, 1, 32, 768), b(4, 4, 1, 64, 640),
        b(3, 1, 2, 80, 1024), b(3, 1, 2, 80, 1024), b(3, 4, 1, 80, 512), b(3, 1, 4, 1, 32, 768), b(3, 4, 4, 1, 16, 640),
        b(3, 1, 1, 80, 512), b(3, 1, 1, 80, 512), b(3, 1, 1, 80, 512), b(3, 1, 1, 1, 32, 768), b(3, 1, 4, 1, 16, 640),
        b(3, 1, 1, 80, 128), b(3, 1, 1, 80, 128), b(3, 1, 1, 80, 128), b(3, 1, 1, 1, 16, 384), b(3, 1, 1, 1, 16, 640),
        v(8, D), v(13, 8, D), v(16, 16, 128), v(16, 16, 128), v(16, 384), v(8, 384),
        pltpu.SemaphoreType.DMA((N_SEM,)), pltpu.SemaphoreType.DMA((N_SEM,)), pltpu.SemaphoreType.DMA,
    ]
    return out


def on_device(tokens_in, cotangent, doc_lengths, w_query, w_key, w_value, w_out, gain_attn_in, gain_attn_out,
              gain_query, gain_key, w_gate, w_up, w_down, gain_ffn_in, gain_ffn_out):
    packed = jnp.concatenate([gain_attn_in, gain_attn_out, gain_query, gain_key, gain_ffn_in, gain_ffn_out])
    packed = jnp.pad(packed, (0, 128 - packed.shape[0])).reshape(1, 128)
    vm = pl.BlockSpec(memory_space=pltpu.VMEM)
    hbm = pl.BlockSpec(memory_space=pl.ANY)
    sm = pl.BlockSpec(memory_space=pltpu.SMEM)

    def s(*shape, dtype=F32):
        return jax.ShapeDtypeStruct(shape, dtype)

    outs = pl.pallas_call(
        kernel,
        out_shape=(
            s(2, 256, D, dtype=BF), s(2, 256, D), s(5, 1024), s(5, 256), s(5, 256), s(8, D), s(5, 2048), s(5, 2048),
            s(16, D), s(1, 5), s(1, 5), s(1, 2), s(1, 2), s(1, 5), s(1, 5),
        ),
        in_specs=[hbm, hbm, sm] + [vm] * 8,
        out_specs=(hbm,) + (vm,) * 14,
        scratch_shapes=scratch(),
        compiler_params=pltpu.CompilerParams(
            collective_id=0, has_side_effects=True, vmem_limit_bytes=64 * 1024 * 1024 - 65536
        ),
        name="block",
    )(tokens_in, cotangent, doc_lengths, packed, w_query, w_key, w_value, w_out, w_gate, w_up, w_down)
    (layer_out, grad_x, gq, gk, gv, go, ggate, gup, gdown, g0, g1, g2, g3, g4, g5) = outs
    return (
        layer_out, grad_x, gq, gk, gv, go, g0.reshape(-1), g1.reshape(-1), g2.reshape(-1), g3.reshape(-1),
        ggate, gup, gdown, g4.reshape(-1), g5.reshape(-1),
    )


def solution(mesh):
    both = ("fsdp", "dp")
    row, gain = P(both, None), P(both)
    tok = P(None, both, None)
    return jax.shard_map(
        on_device,
        mesh=mesh,
        in_specs=(tok, tok, P("fsdp", None, None), row, row, row, row, gain, gain, gain, gain, row, row, row, gain, gain),
        out_specs=(tok, tok, row, row, row, row, gain, gain, gain, gain, row, row, row, gain, gain),
        check_vma=False,
    )
```

```python
import functools
import math

import jax
import jax.numpy as jnp
from jax import lax
from jax.experimental import pallas as pl
from jax.experimental.pallas import tpu as pltpu
from jax.sharding import PartitionSpec as P

MESH = pl.DeviceIdType.MESH
F32 = jnp.float32
BF = jnp.bfloat16
I32 = jnp.int32
EPS = 1e-06
THETA = 1000000.0
T = 512
D = 640
GAINS = ((0, 5, 640), (5, 5, 640), (10, 2, 256), (12, 2, 256), (14, 5, 640), (19, 5, 640))
N_SEM = 96


def mm(a, b):
    return lax.dot_general(a, b, (((1,), (0,)), ((), ())), preferred_element_type=F32)


def mm_nt(a, b):
    return lax.dot_general(a, b, (((1,), (1,)), ((), ())), preferred_element_type=F32)


def mm_tn(a, b):
    return lax.dot_general(a, b, (((0,), (0,)), ((), ())), preferred_element_type=F32)


def mean_last(v):
    return jnp.mean(v, -1, keepdims=True)


def inv_rms(v):
    return lax.rsqrt(mean_last(v * v) + EPS)


def iota(shape, dim):
    return lax.broadcasted_iota(I32, shape, dim)


def norm_back(v, gain, grad):
    r = inv_rms(v)
    hat = v * r
    gg = grad * gain
    return r * (gg - hat * mean_last(gg * hat)), grad * hat


def kernel(
    tok, cot, dl, n0, n1, n2, n3, n4, n5, wq, wk, wv, wo, wg, wu, wd,
    o_layer, o_gx, o_cols, o_rows,
    W1, W2, W3, W4, W5, GW, stf, stage, R1, mf, po, PR, DLB,
    XB, CB, NRM, NRMT, NFT, AMT, CS, SN, DCOL, DROW, GV, QR, Q, KR, KV, AM, LI, OA, LA, BR, HID, NF, GT, UT, HM, ACC, GD, LO,
    DAM, DD, DKV, DKR,
    G2, G3, G4, G5, C1, C2, C3, C4, C5, A1a, A1b, A2, A3, A4, A5, B1a, B1b, B2, B3, B4, B5,
    E1, E2, E3, E4, E5, GG, GGR, F2, c4f, R4, MISC, ss, rs, ls,
):
    f = lax.axis_index("fsdp")
    y = lax.axis_index("dp")
    x = f // 8
    z = (f // 2) % 4
    c = f % 2
    zh, zl = z // 2, z % 2
    me = {"x": x, "z": z, "c": c, "y": y}
    gi = c * 8 + zl * 4 + y
    ge = zl * 8 + c * 4 + y

    def dev(co):
        return ((co["x"] * 4 + co["z"]) * 2 + co["c"], co["y"])

    def member(j):
        return {"x": x, "z": zh * 2 + (j // 4) % 2, "c": j // 8, "y": j % 4}

    def moved(axis, k):
        co = dict(me)
        co[axis] = (me[axis] + k) % (2 if axis == "c" else 4)
        return co

    def near_y():
        return dict(me, y=y + 1 - 2 * (y % 2))

    def under(cond, fn):
        if cond is None:
            fn()
        else:
            pl.when(cond)(fn)

    count = [0]

    def fresh():
        count[0] += 1
        assert count[0] <= N_SEM
        return count[0] - 1

    sent = []

    def remote(src, dst, i, co):
        return pltpu.make_async_remote_copy(
            src_ref=src, dst_ref=dst, send_sem=ss.at[i], recv_sem=rs.at[i], device_id=dev(co), device_id_type=MESH
        )

    def post(copies, come, gone=None):
        i = fresh()
        for cond, src, dst, co in copies:
            under(cond, lambda src=src, dst=dst, co=co: remote(src, dst, i, co).start())
        sent.append((i, come if gone is None else gone))
        return [(i, come)]

    def send(src, dst, co):
        return post([(None, src, dst, co)], [(None, dst)])

    def arrived(batches):
        for i, come in batches:
            for cond, ref in come:
                under(cond, lambda i=i, ref=ref: remote(ref, ref, i, moved("c", 1)).wait_recv())

    def all_gone(batches):
        for i, gone in batches:
            for cond, ref in gone:
                under(cond, lambda i=i, ref=ref: remote(ref, ref, i, moved("c", 1)).wait_send())
        batches.clear()

    def sl_cols(r0, rn):
        def sl(co, done, width=1024):
            xs = slice(None) if "x" in done else pl.ds(co["x"], 1)
            zs = slice(None) if "z" in done else pl.ds(co["z"] // 2, 1)
            if "y" not in done:
                cs, w = co["c"] * 1024 + (co["z"] % 2) * 512 + co["y"] * 128, 128
            elif "z" not in done:
                cs, w = co["c"] * 1024 + (co["z"] % 2) * 512, 512
            else:
                cs, w = co["c"] * 1024, width
            return (xs, zs, pl.ds(r0, rn), pl.ds(pl.multiple_of(cs, 128), w))
        return sl

    def sl_out(co, done):
        xs = slice(None) if "x" in done else pl.ds(co["x"], 1)
        zs = slice(None) if "z" in done else pl.ds(co["z"], 1)
        if "y" in done:
            return (xs, zs, pl.ds(co["c"], 1), pl.ds(0, 32), pl.ds(0, 768))
        return (
            xs, zs, pl.ds(co["c"], 1),
            pl.ds(pl.multiple_of((co["y"] // 2) * 16, 16), 16), pl.ds(pl.multiple_of((co["y"] % 2) * 384, 128), 384),
        )

    def sl_down(co, done):
        xs = slice(None) if "x" in done else pl.ds(co["x"], 1)
        zs = slice(None) if "z" in done else pl.ds(co["z"], 1)
        rows = pl.ds(0, 64) if "y" in done else pl.ds(pl.multiple_of(co["y"] * 16, 16), 16)
        return (xs, zs, pl.ds(co["c"], 1), rows, pl.ds(0, 640))

    pieces = {
        "1": (W1, W2, sl_cols(0, 80), "yzx", (E1, None, None, C1)),
        "1a": (W1, W2, sl_cols(0, 48), "yzx", (None, B1a, A1a, None)),
        "1b": (W1, W2, sl_cols(48, 32), "yxz", (None, B1b, A1b, None)),
        "2": (W2, G2, sl_cols(0, 80), "yzx", (E2, B2, A2, C2)),
        "3": (W3, G3, sl_cols(0, 80), "yxz", (E3, B3, A3, C3)),
        "4": (W4, G4, sl_out, "zxy", (E4, B4, A4, C4)),
        "5": (W5, G5, sl_down, "xzy", (E5, B5, A5, C5)),
    }
    real = jnp.logical_or(c == 0, zl == 0)
    c0, c1 = c == 0, c == 1

    def gather(name, phase):
        w, _, sl, order, bufs = pieces[name]
        done = order[:phase]
        if name[0] == "1" and phase >= 2:
            wide, half = w.at[sl(me, done)], w.at[sl(me, done, 512)]
            if phase == 3:
                to = moved("c", 1)
                return post([(c0, wide, wide, to), (c1, half, half, to)], [(c0, half), (c1, wide)], [(c0, wide), (c1, half)])
            if order[2] == "z":
                ref = w.at[sl(me, done)]
                return post1z(name, phase, ref)
            to = [moved(order[phase], k) for k in (1, 2, 3)]
            b = bufs[phase]
            come = [(c0, b), (c1, b.at[:, :, :, :, pl.ds(0, 512)])]
            return post([(c0, wide, wide, t) for t in to] + [(c1, half, half, t) for t in to], come)
        ref = w.at[sl(me, done)]
        if phase == 3:
            return send(ref, ref, moved("c", 1))
        if name[0] == "1" and order[phase] == "z":
            return post1z(name, phase, ref)
        cond = real if name[0] == "1" else None
        copies = [(cond, ref, ref, moved(order[phase], k)) for k in (1, 2, 3)]
        return post(copies, [(cond, bufs[phase])])

    def post1z(name, phase, ref):
        b = pieces[name][4][phase]
        come = [
            (c0, b), (jnp.logical_and(c1, zl == 0), b.at[pl.ds(0, 1)]), (jnp.logical_and(c1, zl == 1), b.at[pl.ds(0, 2)]),
        ]
        return post([(real, ref, ref, moved("z", k)) for k in (1, 2, 3)], come, [(real, b)])

    bar = pltpu.get_barrier_semaphore()
    friends = [member((gi + d) % 16) for d in range(1, 16)]
    friends += [moved("z", 2)] + [dict(me, z=(zh * 2 + 2) % 4 + (1 - zl))] + [moved("x", k) for k in (1, 2, 3)]
    for co in friends:
        pl.semaphore_signal(bar, inc=1, device_id=dev(co), device_id_type=MESH)

    lane = iota((1, 128), 1)
    grow = jnp.zeros((1, 128), F32)
    for ref, (at, per, _) in zip((n0, n1, n2, n3, n4, n5), GAINS):
        own = ref[...].astype(F32)
        for r in range(per):
            grow = jnp.where(lane == at + r, own[0:1, r:r + 1], grow)
    for j in range(16):
        cols = slice(128 * j, 128 * j + 128)
        if j < 8:
            part = wq[:, cols]
        elif j < 10:
            part = wk[:, 128 * (j - 8):128 * (j - 7)]
        elif j < 12:
            part = wv[:, 128 * (j - 10):128 * (j - 9)]
        else:
            part = None
        stf[j, 0:5, :] = jnp.zeros((5, 128), F32) if part is None else part.astype(F32)
        stf[j, 5:10, :] = wg[:, cols].astype(F32)
        stf[j, 10:15, :] = wu[:, cols].astype(F32)
        stf[j, 15:16, :] = grow
    stage[...] = stf[...].astype(BF)
    wof = wo[...].astype(F32)
    twice = jnp.concatenate([wof, wof], axis=0)
    keep = (iota((16, 640), 0) // 8) == (y % 2)
    twice = jnp.where(keep, twice, 0.0).astype(BF)
    po[0, :, :] = twice[:, 0:384]
    po[1, :, 0:256] = twice[:, 384:640]
    po[1, :, 256:384] = jnp.zeros((16, 128), BF)
    rowid = iota((8, 128), 0)
    tile = jnp.zeros((8, 128), I32)
    for k in range(6):
        tile = jnp.where(rowid == k, dl[0, k // 3:k // 3 + 1, k % 3:k % 3 + 1], tile)
    DLB[c] = tile
    W5[x, z, c, pl.ds(pl.multiple_of(y * 16, 16), 16), :] = wd[...]

    pl.semaphore_wait(bar, len(friends))

    core_to = ((y + 1) // 2) % 2
    blocks = (c, 3 - c)
    micro = y // 2

    def either(v, fn):
        for k in (0, 1):
            pl.when(v == k)(lambda k=k: fn(k))

    def reorder(src, dst, to, mine_in, slot_of):
        i = (fresh(), fresh())
        away = []
        for k in (0, 1):
            own = jnp.logical_and(to[k]["c"] == c, to[k]["y"] == y)
            far = jnp.logical_not(own)

            def start_far(s, k=k):
                pltpu.make_async_remote_copy(
                    src_ref=src.at[k], dst_ref=dst.at[s], send_sem=ss.at[i[k]], recv_sem=rs.at[i[s]],
                    device_id=dev(to[k]), device_id_type=MESH,
                ).start()

            def copy_own(s, k=k):
                cp = pltpu.make_async_copy(src.at[k], dst.at[s], ls)
                cp.start()
                cp.wait()

            for s in (0, 1):
                pl.when(jnp.logical_and(far, slot_of[k] == s))(lambda s=s, f=start_far: f(s))
            for s in (0, 1):
                pl.when(jnp.logical_and(own, slot_of[k] == s))(lambda s=s, f=copy_own: f(s))
            away.append((i[k], [(far, src.at[k])]))
        sent.extend(away)
        return [(i[k], [(jnp.logical_not(mine_in[k]), dst.at[k])]) for k in (0, 1)]

    def reshard(src, dst):
        to = [dict(me, c=core_to, y=c + 2 * m) for m in (0, 1)]
        mine = [jnp.logical_and(blocks[s] == y, c == y % 2) for s in (0, 1)]
        return reorder(src, dst, to, mine, (micro, micro))

    def unshard(src, dst):
        to = [dict(me, c=y % 2, y=blocks[s]) for s in (0, 1)]
        mine = [jnp.logical_and(core_to == c, y == c + 2 * m) for m in (0, 1)]
        return reorder(src, dst, to, mine, (micro, micro))

    others = [(gi + d) % 16 for d in range(1, 16)]
    a2a = post([(None, stage.at[j], R1.at[ge], member(j)) for j in others], [(None, R1.at[pl.ds(0, 15)])])
    R1[ge] = stage[gi]
    pair = send(po.at[1 - y % 2], PR, near_y())
    lens_cp = send(DLB.at[c], DLB.at[c], moved("c", 1))
    g5 = gather("5", 0)

    arrived(a2a)
    for e in range(16):
        v = R1[e].astype(F32)
        for k in range(3):
            mf[k, 5 * e:5 * e + 5, :] = v[5 * k:5 * k + 5, :]
        mf[3, e:e + 1, :] = v[15:16, :]
    own_cols = pl.ds(pl.multiple_of(c * 1024 + zl * 512 + y * 128, 128), 128)
    W1[x, zh, :, own_cols] = mf[0].astype(BF)
    g1 = gather("1", 0)
    GW[x, zh] = mf[3, 0:16, :].astype(BF)
    gz = send(GW.at[x, zh], GW.at[x, zh], moved("z", 2))
    for w, k in ((W2, 1), (W3, 2)):
        w[x, zh, :, own_cols] = mf[k].astype(BF)
    arrived(pair)
    W4[x, z, c, pl.ds(pl.multiple_of((y // 2) * 16, 16), 16), pl.ds(pl.multiple_of((y % 2) * 384, 128), 384)] = (
        po[y % 2].astype(F32) + PR[...].astype(F32)
    ).astype(BF)
    g4, g2, g3 = gather("4", 0), gather("2", 0), gather("3", 0)
    arrived(g1)
    g1a, g1b = gather("1a", 1), gather("1b", 1)
    x_in = reshard(tok, XB)
    arrived(gz)
    gx = post([(None, GW.at[x], GW.at[x], moved("x", k)) for k in (1, 2, 3)], [(None, GW.at[pl.ds(0, 3)])])
    arrived(g5)
    g5 = gather("5", 1)
    arrived(g4)
    g4 = gather("4", 1)
    arrived(g2)
    g2 = gather("2", 1)
    arrived(g3)
    g3 = gather("3", 1)

    def doc_rows():
        lt = DLB[y % 2]
        first = y // 2 == 0
        l0 = jnp.where(first, lt[0:1, :], lt[3:4, :])[:, 0:1]
        l1 = jnp.where(first, lt[1:2, :], lt[4:5, :])[:, 0:1]
        return l0, l0, l1, l0 + l1

    def angles(s):
        l0, e0, l1, e1 = doc_rows()
        freq = jnp.exp(iota((1, 128), 1).astype(F32) * (-2.0 * math.log(THETA) / 256))
        t = blocks[s] * 256 + iota((256, 1), 0)
        p0, p1 = (t >= e0).astype(I32), (t >= e1).astype(I32)
        DCOL[s] = p0 + p1
        turned = (t - p0 * l0 - p1 * l1).astype(F32) * freq
        CS[s] = jnp.cos(turned)
        SN[s] = jnp.sin(turned)

    arrived(lens_cp)
    l0, e0, l1, e1 = doc_rows()
    for k in range(4):
        t = 256 * k + iota((1, 256), 1)
        DROW[k] = (t >= e0).astype(I32) + (t >= e1).astype(I32)
    arrived(g1a + g1b)
    g1a, g1b = gather("1a", 2), gather("1b", 2)
    angles(0)
    arrived(g4)
    g4 = gather("4", 2)
    arrived(gx)

    packed = GW[...].reshape(128, 128)
    for k, (lane, per, width) in enumerate(GAINS):
        col = iota((128, width), 1)
        shard = iota((128, width), 0)
        colf = col.astype(F32)
        rest = colf - per * jnp.floor((colf + 0.5) * (1.0 / per))
        pick = jnp.where(shard.astype(F32) == rest + lane, 1.0, 0.0).astype(BF)
        spread = mm(packed, pick)
        mine = jnp.logical_and(col >= per * shard, col < per * shard + per)
        GV[k:k + 1, 0:width] = jnp.sum(jnp.where(mine, spread, 0.0), 0, keepdims=True)

    def rows(n, fn):
        def step(i, carry):
            fn(pl.ds(pl.multiple_of(i * n, n), n))
            return carry
        lax.fori_loop(0, T // n, step, 0)

    xv = XB.reshape(T, D)
    cv = CB.reshape(T, D)
    csv, snv = CS.reshape(T, 128), SN.reshape(T, 128)

    def do_norm(r):
        v = xv[r, :].astype(F32)
        NRM[r, :] = (v * inv_rms(v) * GV[0:1, :]).astype(BF)
    arrived(x_in)
    rows(128, do_norm)
    arrived(g2)
    g2 = gather("2", 2)
    arrived(g3)
    g3 = gather("3", 2)
    arrived(g5)
    g5 = gather("5", 2)
    NRMT[...] = NRM[...].T
    angles(1)
    arrived(g1a + g1b)
    g1 = gather("1", 3)
    arrived(g1)

    def w1_cols(start, width):
        return W1[:, :, :, pl.ds(pl.multiple_of(start, 128), width)].reshape(D, width)

    def turn(u, cs, sn):
        u1, u2 = u[:, 0:128], u[:, 128:256]
        return u1 * cs - u2 * sn, u2 * cs + u1 * sn

    def turn_back(u, cs, sn):
        u1, u2 = u[:, 0:128], u[:, 128:256]
        return jnp.concatenate([u1 * cs + u2 * sn, u2 * cs - u1 * sn], -1)

    raw = mm(NRM[...], w1_cols(1024, 256))
    KR[...] = raw
    o1, o2 = turn(raw * inv_rms(raw) * GV[3:4, 0:256], csv[...], snv[...])
    vals = mm(NRM[...], w1_cols(1280, 256))
    for s in range(2):
        r = slice(256 * s, 256 * s + 256)
        KV[blocks[s], :, 0:128] = o1[r].astype(BF)
        KV[blocks[s], :, 128:256] = o2[r].astype(BF)
        KV[blocks[s], :, 256:512] = vals[r].astype(BF)
    kv_cp = sum([send(KV.at[blocks[s]], KV.at[blocks[s]], moved("c", 1)) for s in range(2)], [])

    def do_query(h, carry):
        raw = mm(NRM[...], w1_cols(h * 256, 256))
        QR[h] = raw.astype(BF)
        o1, o2 = turn(raw * inv_rms(raw) * GV[2:3, 0:256], csv[...], snv[...])
        for s in range(2):
            r = slice(256 * s, 256 * s + 256)
            Q[s, h, :, 0:128] = (o1[r] * 0.0625).astype(BF)
            Q[s, h, :, 128:256] = (o2[r] * 0.0625).astype(BF)
        return carry
    lax.fori_loop(0, 4, do_query, 0)

    arrived(kv_cp)

    def seen(s, kb):
        t = blocks[s] * 256 + iota((256, 256), 0)
        k = kb * 256 + iota((256, 256), 1)
        return jnp.logical_and(DCOL[s] == DROW[kb], t >= k)

    for s in range(2):
        OA[...] = jnp.zeros_like(OA)
        LA[...] = jnp.zeros_like(LA)

        def forward(kb, carry, s=s):
            vis = seen(s, kb)
            keys, vals = KV[kb, :, 0:256], KV[kb, :, 256:512]
            for h in range(4):
                p = jnp.where(vis, jnp.exp(mm_nt(Q[s, h], keys)), 0.0)
                LA[h] += jnp.sum(p, -1, keepdims=True)
                OA[h] += mm(p.astype(BF), vals)
            return carry
        lax.fori_loop(0, blocks[s] + 1, forward, 0)
        for h in range(4):
            inv = 1.0 / LA[h]
            LI[s, :, h:h + 1] = inv
            mixed = (OA[h] * inv).astype(BF)
            AM[256 * s:256 * s + 256, 256 * h:256 * h + 256] = mixed
            AMT[256 * h:256 * h + 256, 256 * s:256 * s + 256] = mixed.T
    arrived(g4)
    g4 = gather("4", 3)
    c_in = reshard(cot, CB)
    arrived(g4)
    w4v = W4.reshape(1024, 768)
    w5v = W5.reshape(2048, 640)

    def do_out(r):
        b = mm(AM[r, :], w4v[:, 0:640])
        BR[r, :] = b.astype(BF)
        hid = xv[r, :].astype(F32) + b * inv_rms(b) * GV[1:2, :]
        HID[r, :] = hid
        NF[r, :] = (hid * inv_rms(hid) * GV[4:5, :]).astype(BF)
    rows(256, do_out)
    NFT[...] = NF[...].T
    arrived(g2 + g3)
    g2, g3 = gather("2", 3), gather("3", 3)
    arrived(g2 + g3)

    def cols_of(w, at, width):
        return w[:, :, :, pl.ds(pl.multiple_of(at, 128), width)].reshape(D, width)

    def do_ffn(n, carry):
        at = pl.ds(pl.multiple_of(n * 512, 512), 512)
        gate = mm(NF[...], cols_of(W2, n * 512, 512))
        up = mm(NF[...], cols_of(W3, n * 512, 512))
        GT[:, at] = gate.astype(BF)
        UT[:, at] = up.astype(BF)
        HM[:, at] = (jax.nn.gelu(gate, approximate=True) * up).astype(BF)
        return carry
    lax.fori_loop(0, 2, do_ffn, 0)
    arrived(g5)
    g5 = gather("5", 3)
    lax.fori_loop(2, 4, do_ffn, 0)
    arrived(g5)

    arrived(c_in)
    all_gone(sent)
    GG[...] = jnp.zeros_like(GG)
    lov = LO.reshape(T, D)

    def do_down(r):
        d = mm(HM[r, :], w5v[...])
        rd = inv_rms(d)
        hat = d * rd
        lov[r, :] = (HID[r, :] + hat * GV[5:6, :]).astype(BF)
        g = cv[r, :].astype(F32)
        gg = g * GV[5:6, :]
        GD[r, :] = (rd * (gg - hat * mean_last(gg * hat))).astype(BF)
        GG[5:6, :] += jnp.sum(g * hat, 0, keepdims=True)
    rows(256, do_down)
    lo_in = unshard(LO, o_layer)
    lo_sent = list(sent)
    sent.clear()

    def sum_core(name):
        _, g, sl, order, bufs = pieces[name]
        to, buf = moved("c", 1), bufs[3]
        if name == "1":
            part = pl.ds(0, 512)
            small = buf.at[:, :, :, part]
            copies = [(c0, g.at[sl(to, order, 512)], small, to), (c1, g.at[sl(to, order)], buf, to)]
            return post(copies, [(c0, buf), (c1, small)], [(c0, small), (c1, buf)])
        return send(g.at[sl(to, order)], buf, to)

    def add_in(name, idx, bufs, out=None):
        g = pieces[name][1]
        shape = bufs[0].shape
        n1 = shape[1]
        kind = BF if len(bufs) == 1 else F32

        def at(s, k):
            return pl.ds(k if s == slice(None) else s.start + k, 1)

        def step(i, carry):
            here = (at(idx[0], i // n1), at(idx[1], i % n1)) + tuple(idx[2:])
            tot = g[here].astype(kind)
            for b in bufs:
                tot = tot + b[pl.ds(i // n1, 1), pl.ds(i % n1, 1)].astype(kind)
            if out is None:
                g[here] = tot.astype(BF)
            else:
                out(tot)
            return carry
        if shape[0] * n1 == 1:
            step(0, 0)
        else:
            lax.fori_loop(0, shape[0] * n1, step, 0)

    def add_core(name, batch):
        arrived(batch)
        _, _, sl, order, bufs = pieces[name]
        add_in(name, sl(me, order), [bufs[3]])

    def sum_phase(name, phase):
        _, g, sl, order, bufs = pieces[name]
        axis, done, buf = order[phase], order[:phase], bufs[phase]
        peers = [(k, moved(axis, k)) for k in (1, 2, 3)]
        if name[0] == "1" and axis == "z":
            copies = []
            for k, co in peers:
                cond = jnp.logical_or(c0, (z + k) % 2 == 0)
                copies.append((cond, g.at[sl(co, done)], buf.at[k - 1], co))
            gone = [(c0, buf), (jnp.logical_and(c1, zl == 0), buf.at[pl.ds(0, 1)]),
                    (jnp.logical_and(c1, zl == 1), buf.at[pl.ds(0, 2)])]
            return post(copies, [(real, buf)], gone)
        if name[0] == "1" and phase == 2:
            part = pl.ds(0, 512)
            copies = [(c0, g.at[sl(co, done)], buf.at[k - 1], co) for k, co in peers]
            copies += [(c1, g.at[sl(co, done, 512)], buf.at[k - 1, :, :, :, part], co) for k, co in peers]
            return post(copies, [(c0, buf), (c1, buf.at[:, :, :, :, part])])
        cond = real if name[0] == "1" else None
        return post([(cond, g.at[sl(co, done)], buf.at[k - 1], co) for k, co in peers], [(cond, buf)])

    def add_phase(name, phase, batch, out=None):
        arrived(batch)
        _, _, sl, order, bufs = pieces[name]
        add_in(name, sl(me, order[:phase]), [bufs[phase].at[k] for k in range(3)], out)

    g5v = G5.reshape(2048, 640)

    def do_down_grad(n, carry):
        at = pl.ds(pl.multiple_of(n * 512, 512), 512)
        g5v[at, :] = mm_tn(HM[:, at], GD[...]).astype(BF)
        return carry
    lax.fori_loop(0, 4, do_down_grad, 0)
    s5 = sum_core("5")

    def do_ffn_back(n, carry):
        at = pl.ds(pl.multiple_of(n * 512, 512), 512)
        dh = mm_nt(GD[...], w5v[at, :])
        gate, up = GT[:, at].astype(F32), UT[:, at].astype(F32)
        k0, k1 = math.sqrt(2.0 / math.pi), 0.044715
        sq = gate * gate
        th = jnp.tanh(gate * (k0 + k0 * k1 * sq))
        half = 0.5 * (1.0 + th)
        slope = half + (0.5 * gate) * (1.0 - th * th) * (k0 + 3.0 * k0 * k1 * sq)
        dg = (dh * up * slope).astype(BF)
        du = (dh * (gate * half)).astype(BF)
        GT[:, at] = dg
        UT[:, at] = du
        G2[:, :, :, at] = mm(NFT[...], dg).astype(BF).reshape(4, 2, 80, 512)
        G3[:, :, :, at] = mm(NFT[...], du).astype(BF).reshape(4, 2, 80, 512)
        return carry
    lax.fori_loop(0, 1, do_ffn_back, 0)
    add_core("5", s5)
    s5 = sum_phase("5", 2)
    lax.fori_loop(1, 4, do_ffn_back, 0)
    s2, s3 = sum_core("2"), sum_core("3")

    def do_ffn_in(n, carry):
        at = pl.ds(pl.multiple_of(n * 512, 512), 512)
        both = mm_nt(GT[:, at], cols_of(W2, n * 512, 512)) + mm_nt(UT[:, at], cols_of(W3, n * 512, 512))
        if carry is None:
            ACC[...] = both
        else:
            ACC[...] += both
        return carry
    do_ffn_in(0, None)
    add_core("2", s2)
    s2 = sum_phase("2", 2)
    lax.fori_loop(1, 2, do_ffn_in, 0)
    add_core("3", s3)
    s3 = sum_phase("3", 2)
    lax.fori_loop(2, 4, do_ffn_in, 0)

    def do_mid(r):
        g = cv[r, :].astype(F32)
        dv, rowg = norm_back(HID[r, :], GV[4:5, :], ACC[r, :])
        GG[4:5, :] += jnp.sum(rowg, 0, keepdims=True)
        gh = g + dv
        HID[r, :] = gh
        db, rowo = norm_back(BR[r, :].astype(F32), GV[1:2, :], gh)
        GG[1:2, :] += jnp.sum(rowo, 0, keepdims=True)
        GD[r, :] = db.astype(BF)
    rows(128, do_mid)
    g4v = G4.reshape(1024, 768)

    for h in range(4):
        at = slice(256 * h, 256 * h + 256)
        g4v[at, 0:640] = mm(AMT[at, :], GD[...]).astype(BF)
        g4v[at, 640:768] = jnp.zeros((256, 128), BF)
        dam = mm_nt(GD[...], w4v[at, 0:640]).astype(BF)
        inner = jnp.sum(dam.astype(F32) * AM[:, at].astype(F32), -1, keepdims=True)
        for s in range(2):
            r = slice(256 * s, 256 * s + 256)
            DAM[s, h] = dam[r]
            DD[s, :, h:h + 1] = inner[r]
    s4 = sum_core("4")

    DKV[...] = jnp.zeros_like(DKV)
    for s in range(2):
        OA[...] = jnp.zeros_like(OA)

        def backward(kb, carry, s=s, progress={}):
            vis = seen(s, kb)
            keys, vals = KV[kb, :, 0:256], KV[kb, :, 256:512]
            dk = jnp.zeros((256, 256), F32)
            dv = jnp.zeros((256, 256), F32)
            for h in range(4):
                q, da = Q[s, h], DAM[s, h]
                p = jnp.where(vis, jnp.exp(mm_nt(q, keys)) * LI[s, :, h:h + 1], 0.0)
                ds = (p * (mm_nt(da, vals) - DD[s, :, h:h + 1])).astype(BF)
                OA[h] += mm(ds, keys)
                dk = dk + mm_tn(ds, q)
                dv = dv + mm_tn(p.astype(BF), da)
            DKV[kb, :, 0:256] += dk
            DKV[kb, :, 256:512] += dv
            for k, fn in progress.items():
                pl.when(kb == k)(fn)
            return carry
        held = {}

        def early():
            add_core("4", s4)
            held["4"] = sum_phase("4", 2)

        def one():
            add_phase("2", 2, s2)
            held["2"] = sum_phase("2", 1)

        def two():
            add_phase("3", 2, s3)
            held["3"] = sum_phase("3", 1)

        steps = {0: early} if s == 0 else {1: one, 2: two}
        lax.fori_loop(0, blocks[s] + 1, functools.partial(backward, progress=steps), 0)
        if s == 0:
            s4 = held["4"]
            add_phase("5", 2, s5)
            s5 = sum_phase("5", 1)
        else:
            s2, s3 = held["2"], held["3"]

        def query_back(h, carry, s=s):
            dq = turn_back(OA[h] * 0.0625, CS[s], SN[s])
            raw = QR[h, 256 * s:256 * s + 256, :].astype(F32)
            dv, rowg = norm_back(raw, GV[2:3, 0:256], dq)
            GG[2:3, 0:256] += jnp.sum(rowg, 0, keepdims=True)
            GT[256 * s:256 * s + 256, pl.ds(pl.multiple_of(h * 256, 256), 256)] = dv.astype(BF)
            return carry
        lax.fori_loop(0, 4, query_back, 0)
    for s in range(2):
        HM[256 * s:256 * s + 256, 0:512] = DKV[1 - c if s == 0 else 2 + c].astype(BF)
    dk_cp = send(HM.at[:, pl.ds(0, 512)], DKR, moved("c", 1))

    def do_qkv_grad(n, carry):
        at = pl.ds(pl.multiple_of(n * 512, 512), 512)
        W2[:, :, :, at] = mm(NRMT[...], GT[:, at]).astype(BF).reshape(4, 2, 80, 512)
        return carry
    lax.fori_loop(0, 2, do_qkv_grad, 0)
    arrived(dk_cp)
    for s in range(2):
        r = slice(256 * s, 256 * s + 256)
        tot = DKV[blocks[s]] + DKR[r, :].astype(F32)
        dk = turn_back(tot[:, 0:256], CS[s], SN[s])
        dv, rowg = norm_back(KR[r, :], GV[3:4, 0:256], dk)
        GG[3:4, 0:256] += jnp.sum(rowg, 0, keepdims=True)
        GT[r, 1024:1280] = dv.astype(BF)
        GT[r, 1280:1536] = tot[:, 256:512].astype(BF)
    do_qkv_grad(2, 0)
    s1 = sum_core("1")

    def do_dnorm(n, carry):
        at = pl.ds(pl.multiple_of(n * 512, 512), 512)
        part = mm_nt(GT[:, at], w1_cols(n * 512, 512))
        if carry is None:
            ACC[...] = part
        else:
            ACC[...] += part
        return carry
    do_dnorm(0, None)
    add_core("1", s1)
    s1a, s1b = sum_phase("1a", 2), sum_phase("1b", 2)
    add_phase("5", 1, s5)
    s5 = sum_phase("5", 0)
    lax.fori_loop(1, 3, do_dnorm, 0)
    all_gone(lo_sent)
    gxv = LO.reshape(T, D)

    def do_x(r):
        dv, rowg = norm_back(xv[r, :].astype(F32), GV[0:1, :], ACC[r, :])
        GG[0:1, :] += jnp.sum(rowg, 0, keepdims=True)
        gxv[r, :] = (HID[r, :] + dv).astype(BF)
    rows(128, do_x)
    gx_in = unshard(LO, o_gx)
    add_phase("4", 2, s4)
    s4 = sum_phase("4", 1)

    gcp = send(GG, GGR.at[0], moved("c", 1))
    add_phase("2", 1, s2)
    s2 = sum_phase("2", 0)
    add_phase("3", 1, s3)
    s3 = sum_phase("3", 0)

    def out_down(v):
        MISC[0:16, :] = v.reshape(16, 640)
    add_phase("5", 0, s5, out_down)
    arrived(gcp)
    base = 1
    tot = GG[...] + GGR[0]

    def gain_step(a, axis):
        GGR[10 + a] = tot
        return post(
            [(None, GGR.at[10 + a], GGR.at[base + 3 * a + k - 1], moved(axis, k)) for k in (1, 2, 3)],
            [(None, GGR.at[pl.ds(base + 3 * a, 3)])],
        )

    def gain_sum(a, tot):
        for k in range(3):
            tot = tot + GGR[base + 3 * a + k]
        return tot

    gs = gain_step(0, "z")
    add_phase("4", 1, s4)
    s4 = sum_phase("4", 0)
    arrived(gs)
    tot = gain_sum(0, tot)
    gs = gain_step(1, "y")

    add_phase("1a", 2, s1a)
    s1a = sum_phase("1a", 1)
    add_phase("1b", 2, s1b)
    s1b = sum_phase("1b", 1)

    def into(k):
        def out(v):
            mf[k] = v.reshape(80, 128)
        return out

    def out_4(v):
        c4f[...] = v.reshape(16, 384)

    arrived(gs)
    tot = gain_sum(1, tot)
    gs = gain_step(2, "x")
    add_phase("2", 0, s2, into(1))
    add_phase("3", 0, s3, into(2))
    add_phase("4", 0, s4, out_4)
    pair = send(c4f.at[pl.ds(pl.multiple_of(8 * (1 - y % 2), 8), 8), :], R4, near_y())
    for e in range(16):
        for k in (1, 2):
            F2[e, 5 * k:5 * k + 5, :] = mf[k, 5 * e:5 * e + 5, :]
    add_phase("1a", 1, s1a)
    add_phase("1b", 1, s1b)
    s1 = sum_phase("1", 0)
    arrived(gs)
    tot = gain_sum(2, tot)
    shard = f * 4 + y
    MISC[24:32, :] = jnp.zeros((8, D), F32)
    for k, (_, per, width) in enumerate(GAINS):
        line = tot[k:k + 1, 0:width]
        col = iota((1, width), 1)
        for r in range(per):
            MISC[24 + k:25 + k, r:r + 1] = jnp.sum(jnp.where(col == per * shard + r, line, 0.0), 1, keepdims=True)
    arrived(pair)
    own = c4f[pl.ds(pl.multiple_of(8 * (y % 2), 8), 8), :]
    left = y % 2 == 0
    MISC[16:24, 0:384] = jnp.where(left, own, R4[...])
    MISC[16:24, 384:640] = jnp.where(left, R4[...], own)[:, 0:256]
    keep_rows = pltpu.make_async_copy(MISC, o_rows, ls)
    keep_rows.start()
    keep_rows.wait()
    add_phase("1", 0, s1, into(0))
    for e in range(16):
        F2[e, 0:5, :] = mf[0, 5 * e:5 * e + 5, :]
    home = post(
        [(None, F2.at[(j // 4) % 2 * 8 + j // 8 * 4 + j % 4], o_cols.at[gi], member(j)) for j in others],
        [(None, o_cols.at[pl.ds(0, 15)])],
    )
    keep_cols = pltpu.make_async_copy(F2.at[ge], o_cols.at[gi], ls)
    keep_cols.start()
    keep_cols.wait()
    arrived(gx_in + lo_in + home)
    all_gone(sent)


def finish(lay, gx, cols, rows, o_layer, o_gx, o_q, o_k, o_v, o_o, o_gate, o_up, o_down, o0, o1, o2, o3, o4, o5):
    o_layer[...] = lay[...]
    for j in range(16):
        at = slice(128 * j, 128 * j + 128)
        v = cols[j]
        if j < 8:
            o_q[:, at] = v[0:5]
        elif j < 10:
            o_k[:, 128 * (j - 8):128 * (j - 7)] = v[0:5]
        elif j < 12:
            o_v[:, 128 * (j - 10):128 * (j - 9)] = v[0:5]
        o_gate[:, at] = v[5:10]
        o_up[:, at] = v[10:15]
    o_down[...] = rows[0:16, :]
    o_o[...] = rows[16:24, :]
    for k, ref in enumerate((o0, o1, o2, o3, o4, o5)):
        ref[...] = rows[24 + k:25 + k, 0:GAINS[k][1]]
    for m in range(2):
        o_gx[m] = gx[m].astype(F32)


def scratch():
    def v(*shape, dtype=F32):
        return pltpu.VMEM(shape, dtype)

    def b(*shape):
        return pltpu.VMEM(shape, BF)

    cols = (4, 2, 80, 2048)
    out = [
        b(*cols), b(*cols), b(*cols), b(4, 4, 2, 32, 768), b(4, 4, 2, 64, 640), b(4, 2, 16, 128),
        v(16, 16, 128), b(16, 16, 128), b(16, 16, 128), v(4, 80, 128), b(2, 16, 384), b(16, 384),
        v(2, 8, 128, dtype=I32),
        b(2, 256, D), b(2, 256, D), b(T, D), b(D, T), b(D, T), b(1024, T),
        v(2, 256, 128), v(2, 256, 128),
        v(2, 256, 1, dtype=I32), v(4, 1, 256, dtype=I32), v(8, D),
        b(4, T, 256), b(2, 4, 256, 256), v(T, 256), b(4, 256, 512), b(T, 1024),
        v(2, 256, 4), v(4, 256, 256), v(4, 256, 1),
        b(T, D), v(T, D), b(T, D), b(T, 2048), b(T, 2048), b(T, 2048), v(T, D), b(T, D),
        b(2, 256, D),
        b(2, 4, 256, 256), v(2, 256, 4), v(4, 256, 512), b(T, 512),
        b(*cols), b(*cols), b(4, 4, 2, 32, 768), b(4, 4, 2, 64, 640),
        b(4, 2, 80, 1024), b(4, 2, 80, 1024), b(4, 2, 80, 1024), b(4, 4, 1, 32, 768), b(4, 4, 1, 64, 640),
        b(3, 1, 2, 48, 1024), b(3, 4, 1, 32, 512), b(3, 1, 2, 80, 1024), b(3, 4, 1, 80, 512),
        b(3, 4, 4, 1, 16, 384), b(3, 4, 4, 1, 16, 640),
        b(3, 1, 1, 48, 512), b(3, 1, 1, 32, 512), b(3, 1, 1, 80, 512), b(3, 1, 1, 80, 512),
        b(3, 1, 4, 1, 16, 384), b(3, 4, 1, 1, 16, 640),
        b(3, 1, 1, 80, 128), b(3, 1, 1, 80, 128), b(3, 1, 1, 80, 128), b(3, 1, 1, 1, 16, 384), b(3, 1, 1, 1, 16, 640),
        v(8, D), v(13, 8, D), v(16, 16, 128), v(16, 384), v(8, 384), v(32, D),
        pltpu.SemaphoreType.DMA((N_SEM,)), pltpu.SemaphoreType.DMA((N_SEM,)), pltpu.SemaphoreType.DMA,
    ]
    return out


def on_device(tokens_in, cotangent, doc_lengths, w_query, w_key, w_value, w_out, gain_attn_in, gain_attn_out,
              gain_query, gain_key, w_gate, w_up, w_down, gain_ffn_in, gain_ffn_out):
    gains = [g.reshape(1, -1) for g in (gain_attn_in, gain_attn_out, gain_query, gain_key, gain_ffn_in, gain_ffn_out)]
    vm = pl.BlockSpec(memory_space=pltpu.VMEM)
    hbm = pl.BlockSpec(memory_space=pl.ANY)

    def s(*shape, dtype=F32):
        return jax.ShapeDtypeStruct(shape, dtype)

    parts = pl.pallas_call(
        kernel,
        out_shape=(s(2, 256, D, dtype=BF), s(2, 256, D, dtype=BF), s(16, 16, 128), s(32, D)),
        in_specs=[hbm, hbm] + [vm] * 14,
        out_specs=(hbm,) * 4,
        scratch_shapes=scratch(),
        compiler_params=pltpu.CompilerParams(
            collective_id=0, has_side_effects=True, vmem_limit_bytes=64 * 1024 * 1024 - 65536
        ),
        name="block",
    )(tokens_in, cotangent, doc_lengths, *gains, w_query, w_key, w_value, w_out, w_gate, w_up, w_down)
    outs = pl.pallas_call(
        finish,
        out_shape=(
            s(2, 256, D, dtype=BF), s(2, 256, D), s(5, 1024), s(5, 256), s(5, 256), s(8, D), s(5, 2048), s(5, 2048),
            s(16, D), s(1, 5), s(1, 5), s(1, 2), s(1, 2), s(1, 5), s(1, 5),
        ),
        in_specs=[vm] * 4,
        out_specs=(vm,) * 15,
        name="finish",
    )(*parts)
    (layer_out, grad_x, gq, gk, gv, go, ggate, gup, gdown, g0, g1, g2, g3, g4, g5) = outs
    return (
        layer_out, grad_x, gq, gk, gv, go, g0.reshape(-1), g1.reshape(-1), g2.reshape(-1), g3.reshape(-1),
        ggate, gup, gdown, g4.reshape(-1), g5.reshape(-1),
    )


def solution(mesh):
    both = ("fsdp", "dp")
    row, gain = P(both, None), P(both)
    tok = P(None, both, None)
    return jax.shard_map(
        on_device,
        mesh=mesh,
        in_specs=(tok, tok, P("fsdp", None, None), row, row, row, row, gain, gain, gain, gain, row, row, row, gain, gain),
        out_specs=(tok, tok, row, row, row, row, gain, gain, gain, gain, row, row, row, gain, gain),
        check_vma=False,
    )
```

```python
import functools
import math

import jax
import jax.numpy as jnp
from jax import lax
from jax.experimental import pallas as pl
from jax.experimental.pallas import tpu as pltpu
from jax.sharding import PartitionSpec as P

MESH = pl.DeviceIdType.MESH
F32 = jnp.float32
BF = jnp.bfloat16
I32 = jnp.int32
EPS = 1e-06
THETA = 1000000.0
T = 512
D = 640
GAINS = ((0, 5, 640), (5, 5, 640), (10, 2, 256), (12, 2, 256), (14, 5, 640), (19, 5, 640))
N_SEM = 96


def mm(a, b):
    return lax.dot_general(a, b, (((1,), (0,)), ((), ())), preferred_element_type=F32)


def mm_nt(a, b):
    return lax.dot_general(a, b, (((1,), (1,)), ((), ())), preferred_element_type=F32)


def mm_tn(a, b):
    return lax.dot_general(a, b, (((0,), (0,)), ((), ())), preferred_element_type=F32)


def mean_last(v):
    return jnp.mean(v, -1, keepdims=True)


def inv_rms(v):
    return lax.rsqrt(mean_last(v * v) + EPS)


def iota(shape, dim):
    return lax.broadcasted_iota(I32, shape, dim)


def norm_back(v, gain, grad):
    r = inv_rms(v)
    hat = v * r
    gg = grad * gain
    return r * (gg - hat * mean_last(gg * hat)), grad * hat


def kernel(
    tok, cot, dl, n0, n1, n2, n3, n4, n5, wq, wk, wv, wo, wg, wu, wd,
    o_layer, o_gx, o_cols, o_rows,
    W1, W2, W3, W4, W5, GW, stf, stage, R1, mf, po, PR, DLB,
    XB, CB, NRM, NRMT, NFT, AMT, CS, SN, DCOL, DROW, GV, QR, Q, KR, KV, AM, LI, OA, LA, BR, HID, NF, GT, UT, HM, ACC, GD, LO,
    DAM, DD, DKV, DKR,
    G2, G3, G4, G5, C1, C2, C3, C4, C5, A1a, A1b, A2, A3, A4, A5, B1a, B1b, B2, B3, B4, B5,
    E1, E2, E3, E4, E5, GG, GGR, F2, c4f, R4, MISC, ss, rs, ls,
):
    f = lax.axis_index("fsdp")
    y = lax.axis_index("dp")
    x = f // 8
    z = (f // 2) % 4
    c = f % 2
    zh, zl = z // 2, z % 2
    me = {"x": x, "z": z, "c": c, "y": y}
    gi = c * 8 + zl * 4 + y
    ge = zl * 8 + c * 4 + y

    def dev(co):
        return ((co["x"] * 4 + co["z"]) * 2 + co["c"], co["y"])

    def member(j):
        return {"x": x, "z": zh * 2 + (j // 4) % 2, "c": j // 8, "y": j % 4}

    def moved(axis, k):
        co = dict(me)
        co[axis] = (me[axis] + k) % (2 if axis == "c" else 4)
        return co

    def near_y():
        return dict(me, y=y + 1 - 2 * (y % 2))

    def under(cond, fn):
        if cond is None:
            fn()
        else:
            pl.when(cond)(fn)

    count = [0]

    def fresh():
        count[0] += 1
        assert count[0] <= N_SEM
        return count[0] - 1

    sent = []

    def remote(src, dst, i, co):
        return pltpu.make_async_remote_copy(
            src_ref=src, dst_ref=dst, send_sem=ss.at[i], recv_sem=rs.at[i], device_id=dev(co), device_id_type=MESH
        )

    def post(copies, come, gone=None):
        i = fresh()
        for cond, src, dst, co in copies:
            under(cond, lambda src=src, dst=dst, co=co: remote(src, dst, i, co).start())
        sent.append((i, come if gone is None else gone))
        return [(i, come)]

    def send(src, dst, co):
        return post([(None, src, dst, co)], [(None, dst)])

    def arrived(batches):
        for i, come in batches:
            for cond, ref in come:
                under(cond, lambda i=i, ref=ref: remote(ref, ref, i, moved("c", 1)).wait_recv())

    def all_gone(batches):
        for i, gone in batches:
            for cond, ref in gone:
                under(cond, lambda i=i, ref=ref: remote(ref, ref, i, moved("c", 1)).wait_send())
        batches.clear()

    def sl_cols(r0, rn):
        def sl(co, done, width=1024):
            xs = slice(None) if "x" in done else pl.ds(co["x"], 1)
            zs = slice(None) if "z" in done else pl.ds(co["z"] // 2, 1)
            if "y" not in done:
                cs, w = co["c"] * 1024 + (co["z"] % 2) * 512 + co["y"] * 128, 128
            elif "z" not in done:
                cs, w = co["c"] * 1024 + (co["z"] % 2) * 512, 512
            else:
                cs, w = co["c"] * 1024, width
            return (xs, zs, pl.ds(r0, rn), pl.ds(pl.multiple_of(cs, 128), w))
        return sl

    def sl_out(co, done):
        xs = slice(None) if "x" in done else pl.ds(co["x"], 1)
        zs = slice(None) if "z" in done else pl.ds(co["z"], 1)
        if "y" in done:
            return (xs, zs, pl.ds(co["c"], 1), pl.ds(0, 32), pl.ds(0, 768))
        return (
            xs, zs, pl.ds(co["c"], 1),
            pl.ds(pl.multiple_of((co["y"] // 2) * 16, 16), 16), pl.ds(pl.multiple_of((co["y"] % 2) * 384, 128), 384),
        )

    def sl_down(co, done):
        xs = slice(None) if "x" in done else pl.ds(co["x"], 1)
        zs = slice(None) if "z" in done else pl.ds(co["z"], 1)
        rows = pl.ds(0, 64) if "y" in done else pl.ds(pl.multiple_of(co["y"] * 16, 16), 16)
        return (xs, zs, pl.ds(co["c"], 1), rows, pl.ds(0, 640))

    pieces = {
        "1": (W1, W2, sl_cols(0, 80), "yzx", (E1, None, None, C1)),
        "1a": (W1, W2, sl_cols(0, 48), "yzx", (None, B1a, A1a, None)),
        "1b": (W1, W2, sl_cols(48, 32), "yxz", (None, B1b, A1b, None)),
        "2": (W2, G2, sl_cols(0, 80), "yzx", (E2, B2, A2, C2)),
        "3": (W3, G3, sl_cols(0, 80), "yxz", (E3, B3, A3, C3)),
        "4": (W4, G4, sl_out, "zxy", (E4, B4, A4, C4)),
        "5": (W5, G5, sl_down, "xzy", (E5, B5, A5, C5)),
    }
    real = jnp.logical_or(c == 0, zl == 0)
    c0, c1 = c == 0, c == 1

    def gather(name, phase):
        w, _, sl, order, bufs = pieces[name]
        done = order[:phase]
        if name[0] == "1" and phase >= 2:
            wide, half = w.at[sl(me, done)], w.at[sl(me, done, 512)]
            if phase == 3:
                to = moved("c", 1)
                return post([(c0, wide, wide, to), (c1, half, half, to)], [(c0, half), (c1, wide)], [(c0, wide), (c1, half)])
            if order[2] == "z":
                ref = w.at[sl(me, done)]
                return post1z(name, phase, ref)
            to = [moved(order[phase], k) for k in (1, 2, 3)]
            b = bufs[phase]
            come = [(c0, b), (c1, b.at[:, :, :, :, pl.ds(0, 512)])]
            return post([(c0, wide, wide, t) for t in to] + [(c1, half, half, t) for t in to], come)
        ref = w.at[sl(me, done)]
        if phase == 3:
            return send(ref, ref, moved("c", 1))
        if name[0] == "1" and order[phase] == "z":
            return post1z(name, phase, ref)
        cond = real if name[0] == "1" else None
        copies = [(cond, ref, ref, moved(order[phase], k)) for k in (1, 2, 3)]
        return post(copies, [(cond, bufs[phase])])

    def ring(name, step):
        w, _, sl, order, bufs = pieces[name]
        axis, done, buf = order[2], order[:2], bufs[2]
        right, left = moved(axis, 1), moved(axis, 3)
        if step == 0:
            ref = w.at[sl(me, done)]
            return post([(None, ref, ref, right), (None, ref, ref, left)], [(None, buf.at[pl.ds(0, 2)])])

        def half(co, k):
            at = sl(co, done)
            n = at[3].size // 2
            return w.at[at[:3] + (pl.ds(pl.multiple_of(at[3].start + k * n, 128), n),)]
        one, two = half(left, 0), half(right, 1)
        return post([(None, one, one, right), (None, two, two, left)], [(None, buf.at[pl.ds(0, 1)])])

    def post1z(name, phase, ref):
        b = pieces[name][4][phase]
        come = [
            (c0, b), (jnp.logical_and(c1, zl == 0), b.at[pl.ds(0, 1)]), (jnp.logical_and(c1, zl == 1), b.at[pl.ds(0, 2)]),
        ]
        return post([(real, ref, ref, moved("z", k)) for k in (1, 2, 3)], come, [(real, b)])

    bar = pltpu.get_barrier_semaphore()
    friends = [member((gi + d) % 16) for d in range(1, 16)]
    friends += [moved("z", 2)] + [dict(me, z=(zh * 2 + 2) % 4 + (1 - zl))] + [moved("x", k) for k in (1, 2, 3)]
    for co in friends:
        pl.semaphore_signal(bar, inc=1, device_id=dev(co), device_id_type=MESH)

    lane = iota((1, 128), 1)
    grow = jnp.zeros((1, 128), F32)
    for ref, (at, per, _) in zip((n0, n1, n2, n3, n4, n5), GAINS):
        own = ref[...].astype(F32)
        for r in range(per):
            grow = jnp.where(lane == at + r, own[0:1, r:r + 1], grow)
    for j in range(16):
        cols = slice(128 * j, 128 * j + 128)
        if j < 8:
            part = wq[:, cols]
        elif j < 10:
            part = wk[:, 128 * (j - 8):128 * (j - 7)]
        elif j < 12:
            part = wv[:, 128 * (j - 10):128 * (j - 9)]
        else:
            part = None
        stf[j, 0:5, :] = jnp.zeros((5, 128), F32) if part is None else part.astype(F32)
        stf[j, 5:10, :] = wg[:, cols].astype(F32)
        stf[j, 10:15, :] = wu[:, cols].astype(F32)
        stf[j, 15:16, :] = grow
    stage[...] = stf[...].astype(BF)
    wof = wo[...].astype(F32)
    twice = jnp.concatenate([wof, wof], axis=0)
    keep = (iota((16, 640), 0) // 8) == (y % 2)
    twice = jnp.where(keep, twice, 0.0).astype(BF)
    po[0, :, :] = twice[:, 0:384]
    po[1, :, 0:256] = twice[:, 384:640]
    po[1, :, 256:384] = jnp.zeros((16, 128), BF)
    rowid = iota((8, 128), 0)
    tile = jnp.zeros((8, 128), I32)
    for k in range(6):
        tile = jnp.where(rowid == k, dl[0, k // 3:k // 3 + 1, k % 3:k % 3 + 1], tile)
    DLB[c] = tile
    W5[x, z, c, pl.ds(pl.multiple_of(y * 16, 16), 16), :] = wd[...]

    pl.semaphore_wait(bar, len(friends))

    core_to = ((y + 1) // 2) % 2
    blocks = (c, 3 - c)
    micro = y // 2

    def either(v, fn):
        for k in (0, 1):
            pl.when(v == k)(lambda k=k: fn(k))

    def reorder(src, dst, to, mine_in, slot_of):
        i = (fresh(), fresh())
        away = []
        for k in (0, 1):
            own = jnp.logical_and(to[k]["c"] == c, to[k]["y"] == y)
            far = jnp.logical_not(own)

            def start_far(s, k=k):
                pltpu.make_async_remote_copy(
                    src_ref=src.at[k], dst_ref=dst.at[s], send_sem=ss.at[i[k]], recv_sem=rs.at[i[s]],
                    device_id=dev(to[k]), device_id_type=MESH,
                ).start()

            def copy_own(s, k=k):
                cp = pltpu.make_async_copy(src.at[k], dst.at[s], ls)
                cp.start()
                cp.wait()

            for s in (0, 1):
                pl.when(jnp.logical_and(far, slot_of[k] == s))(lambda s=s, f=start_far: f(s))
            for s in (0, 1):
                pl.when(jnp.logical_and(own, slot_of[k] == s))(lambda s=s, f=copy_own: f(s))
            away.append((i[k], [(far, src.at[k])]))
        sent.extend(away)
        return [(i[k], [(jnp.logical_not(mine_in[k]), dst.at[k])]) for k in (0, 1)]

    def reshard(src, dst):
        to = [dict(me, c=core_to, y=c + 2 * m) for m in (0, 1)]
        mine = [jnp.logical_and(blocks[s] == y, c == y % 2) for s in (0, 1)]
        return reorder(src, dst, to, mine, (micro, micro))

    def unshard(src, dst):
        to = [dict(me, c=y % 2, y=blocks[s]) for s in (0, 1)]
        mine = [jnp.logical_and(core_to == c, y == c + 2 * m) for m in (0, 1)]
        return reorder(src, dst, to, mine, (micro, micro))

    others = [(gi + d) % 16 for d in range(1, 16)]
    a2a = post([(None, stage.at[j], R1.at[ge], member(j)) for j in others], [(None, R1.at[pl.ds(0, 15)])])
    R1[ge] = stage[gi]
    pair = send(po.at[1 - y % 2], PR, near_y())
    lens_cp = send(DLB.at[c], DLB.at[c], moved("c", 1))
    g5 = gather("5", 0)

    arrived(a2a)
    for e in range(16):
        v = R1[e].astype(F32)
        for k in range(3):
            mf[k, 5 * e:5 * e + 5, :] = v[5 * k:5 * k + 5, :]
        mf[3, e:e + 1, :] = v[15:16, :]
    own_cols = pl.ds(pl.multiple_of(c * 1024 + zl * 512 + y * 128, 128), 128)
    W1[x, zh, :, own_cols] = mf[0].astype(BF)
    g1 = gather("1", 0)
    GW[x, zh] = mf[3, 0:16, :].astype(BF)
    gz = send(GW.at[x, zh], GW.at[x, zh], moved("z", 2))
    for w, k in ((W2, 1), (W3, 2)):
        w[x, zh, :, own_cols] = mf[k].astype(BF)
    arrived(pair)
    W4[x, z, c, pl.ds(pl.multiple_of((y // 2) * 16, 16), 16), pl.ds(pl.multiple_of((y % 2) * 384, 128), 384)] = (
        po[y % 2].astype(F32) + PR[...].astype(F32)
    ).astype(BF)
    g4, g2, g3 = gather("4", 0), gather("2", 0), gather("3", 0)
    arrived(g1)
    g1a, g1b = gather("1a", 1), gather("1b", 1)
    x_in = reshard(tok, XB)
    arrived(gz)
    gx = post([(None, GW.at[x], GW.at[x], moved("x", k)) for k in (1, 2, 3)], [(None, GW.at[pl.ds(0, 3)])])
    arrived(g1a)
    g1a = gather("1a", 2)
    arrived(g1b)
    g1b = gather("1b", 2)
    arrived(g4)
    g4 = gather("4", 1)
    arrived(g2)
    g2 = gather("2", 1)
    arrived(g3)
    g3 = gather("3", 1)
    arrived(g5)
    g5 = gather("5", 1)

    def doc_rows():
        lt = DLB[y % 2]
        first = y // 2 == 0
        l0 = jnp.where(first, lt[0:1, :], lt[3:4, :])[:, 0:1]
        l1 = jnp.where(first, lt[1:2, :], lt[4:5, :])[:, 0:1]
        return l0, l0, l1, l0 + l1

    def angles(s):
        l0, e0, l1, e1 = doc_rows()
        freq = jnp.exp(iota((1, 128), 1).astype(F32) * (-2.0 * math.log(THETA) / 256))
        t = blocks[s] * 256 + iota((256, 1), 0)
        p0, p1 = (t >= e0).astype(I32), (t >= e1).astype(I32)
        DCOL[s] = p0 + p1
        turned = (t - p0 * l0 - p1 * l1).astype(F32) * freq
        CS[s] = jnp.cos(turned)
        SN[s] = jnp.sin(turned)

    arrived(lens_cp)
    l0, e0, l1, e1 = doc_rows()
    for k in range(4):
        t = 256 * k + iota((1, 256), 1)
        DROW[k] = (t >= e0).astype(I32) + (t >= e1).astype(I32)
    angles(0)
    angles(1)
    arrived(gx)

    packed = GW[...].reshape(128, 128)
    for k, (lane, per, width) in enumerate(GAINS):
        col = iota((128, width), 1)
        shard = iota((128, width), 0)
        colf = col.astype(F32)
        rest = colf - per * jnp.floor((colf + 0.5) * (1.0 / per))
        pick = jnp.where(shard.astype(F32) == rest + lane, 1.0, 0.0).astype(BF)
        spread = mm(packed, pick)
        mine = jnp.logical_and(col >= per * shard, col < per * shard + per)
        GV[k:k + 1, 0:width] = jnp.sum(jnp.where(mine, spread, 0.0), 0, keepdims=True)

    def rows(n, fn):
        def step(i, carry):
            fn(pl.ds(pl.multiple_of(i * n, n), n))
            return carry
        lax.fori_loop(0, T // n, step, 0)

    xv = XB.reshape(T, D)
    cv = CB.reshape(T, D)
    csv, snv = CS.reshape(T, 128), SN.reshape(T, 128)

    def do_norm(r):
        v = xv[r, :].astype(F32)
        NRM[r, :] = (v * inv_rms(v) * GV[0:1, :]).astype(BF)
    arrived(x_in)
    rows(128, do_norm)
    arrived(g4)
    g4 = gather("4", 2)
    arrived(g1a + g1b)
    g1 = gather("1", 3)
    arrived(g2)
    g2 = ring("2", 0)
    arrived(g3)
    g3 = ring("3", 0)
    arrived(g5)
    g5 = gather("5", 2)
    NRMT[...] = NRM[...].T
    arrived(g1)

    def w1_cols(start, width):
        return W1[:, :, :, pl.ds(pl.multiple_of(start, 128), width)].reshape(D, width)

    def turn(u, cs, sn):
        u1, u2 = u[:, 0:128], u[:, 128:256]
        return u1 * cs - u2 * sn, u2 * cs + u1 * sn

    def turn_back(u, cs, sn):
        u1, u2 = u[:, 0:128], u[:, 128:256]
        return jnp.concatenate([u1 * cs + u2 * sn, u2 * cs - u1 * sn], -1)

    raw = mm(NRM[...], w1_cols(1024, 256))
    KR[...] = raw
    o1, o2 = turn(raw * inv_rms(raw) * GV[3:4, 0:256], csv[...], snv[...])
    vals = mm(NRM[...], w1_cols(1280, 256))
    for s in range(2):
        r = slice(256 * s, 256 * s + 256)
        KV[blocks[s], :, 0:128] = o1[r].astype(BF)
        KV[blocks[s], :, 128:256] = o2[r].astype(BF)
        KV[blocks[s], :, 256:512] = vals[r].astype(BF)
    kv_cp = sum([send(KV.at[blocks[s]], KV.at[blocks[s]], moved("c", 1)) for s in range(2)], [])

    def do_query(h, carry):
        raw = mm(NRM[...], w1_cols(h * 256, 256))
        QR[h] = raw.astype(BF)
        o1, o2 = turn(raw * inv_rms(raw) * GV[2:3, 0:256], csv[...], snv[...])
        for s in range(2):
            r = slice(256 * s, 256 * s + 256)
            Q[s, h, :, 0:128] = (o1[r] * 0.0625).astype(BF)
            Q[s, h, :, 128:256] = (o2[r] * 0.0625).astype(BF)
        return carry
    lax.fori_loop(0, 4, do_query, 0)

    arrived(kv_cp)

    def seen(s, kb):
        t = blocks[s] * 256 + iota((256, 256), 0)
        k = kb * 256 + iota((256, 256), 1)
        return jnp.logical_and(DCOL[s] == DROW[kb], t >= k)

    for s in range(2):
        OA[...] = jnp.zeros_like(OA)
        LA[...] = jnp.zeros_like(LA)

        def forward(kb, carry, s=s, progress={}):
            vis = seen(s, kb)
            keys, vals = KV[kb, :, 0:256], KV[kb, :, 256:512]
            for h in range(4):
                p = jnp.where(vis, jnp.exp(mm_nt(Q[s, h], keys)), 0.0)
                LA[h] += jnp.sum(p, -1, keepdims=True)
                OA[h] += mm(p.astype(BF), vals)
            for k, fn in progress.items():
                pl.when(kb == k)(fn)
            return carry
        held = {}

        def core_four():
            arrived(g4)
            held["4"] = gather("4", 3)

        def pass_on():
            arrived(g2 + g3)
            held["2"], held["3"] = ring("2", 1), ring("3", 1)

        steps = {} if s == 0 else {1: core_four, 2: pass_on}
        lax.fori_loop(0, blocks[s] + 1, functools.partial(forward, progress=steps), 0)
        for h in range(4):
            inv = 1.0 / LA[h]
            LI[s, :, h:h + 1] = inv
            mixed = (OA[h] * inv).astype(BF)
            AM[256 * s:256 * s + 256, 256 * h:256 * h + 256] = mixed
            AMT[256 * h:256 * h + 256, 256 * s:256 * s + 256] = mixed.T
    g4, g2, g3 = held["4"], held["2"], held["3"]
    c_in = reshard(cot, CB)
    arrived(g2 + g3)
    g2, g3 = gather("2", 3), gather("3", 3)
    arrived(g4)
    w4v = W4.reshape(1024, 768)
    w5v = W5.reshape(2048, 640)

    def do_out(r):
        b = mm(AM[r, :], w4v[:, 0:640])
        BR[r, :] = b.astype(BF)
        hid = xv[r, :].astype(F32) + b * inv_rms(b) * GV[1:2, :]
        HID[r, :] = hid
        NF[r, :] = (hid * inv_rms(hid) * GV[4:5, :]).astype(BF)
    rows(256, do_out)
    NFT[...] = NF[...].T
    arrived(g2 + g3)

    def cols_of(w, at, width):
        return w[:, :, :, pl.ds(pl.multiple_of(at, 128), width)].reshape(D, width)

    def do_ffn(n, carry):
        at = pl.ds(pl.multiple_of(n * 512, 512), 512)
        gate = mm(NF[...], cols_of(W2, n * 512, 512))
        up = mm(NF[...], cols_of(W3, n * 512, 512))
        GT[:, at] = gate.astype(BF)
        UT[:, at] = up.astype(BF)
        HM[:, at] = (jax.nn.gelu(gate, approximate=True) * up).astype(BF)
        return carry
    lax.fori_loop(0, 2, do_ffn, 0)
    arrived(g5)
    g5 = gather("5", 3)
    lax.fori_loop(2, 4, do_ffn, 0)
    arrived(g5)

    arrived(c_in)
    all_gone(sent)
    GG[...] = jnp.zeros_like(GG)
    lov = LO.reshape(T, D)

    def do_down(r):
        d = mm(HM[r, :], w5v[...])
        rd = inv_rms(d)
        hat = d * rd
        lov[r, :] = (HID[r, :] + hat * GV[5:6, :]).astype(BF)
        g = cv[r, :].astype(F32)
        gg = g * GV[5:6, :]
        GD[r, :] = (rd * (gg - hat * mean_last(gg * hat))).astype(BF)
        GG[5:6, :] += jnp.sum(g * hat, 0, keepdims=True)
    rows(256, do_down)
    lo_in = unshard(LO, o_layer)
    lo_sent = list(sent)
    sent.clear()

    def sum_core(name, half=None):
        _, g, sl, order, bufs = pieces[name]
        to, buf = moved("c", 1), bufs[3]
        if half == 0:
            return post([(c1, g.at[sl(to, order)], buf, to)], [(c0, buf)], [(c1, buf)])
        if half == 1:
            wide = 512 if name == "1" else 1024
            buf = buf.at[:, :, :, pl.ds(0, wide)]
            return post([(c0, g.at[sl(to, order, wide)], buf, to)], [(c1, buf)], [(c0, buf)])
        return send(g.at[sl(to, order)], buf, to)

    def add_in(name, idx, bufs, out=None):
        g = pieces[name][1]
        shape = bufs[0].shape
        n1 = shape[1]
        kind = BF if len(bufs) == 1 else F32

        def at(s, k):
            return pl.ds(k if s == slice(None) else s.start + k, 1)

        def step(i, carry):
            here = (at(idx[0], i // n1), at(idx[1], i % n1)) + tuple(idx[2:])
            tot = g[here].astype(kind)
            for b in bufs:
                tot = tot + b[pl.ds(i // n1, 1), pl.ds(i % n1, 1)].astype(kind)
            if out is None:
                g[here] = tot.astype(BF)
            else:
                out(tot)
            return carry
        if shape[0] * n1 == 1:
            step(0, 0)
        else:
            lax.fori_loop(0, shape[0] * n1, step, 0)

    def add_core(name, batch, half=None):
        arrived(batch)
        _, _, sl, order, bufs = pieces[name]
        under(None if half is None else c == half, lambda: add_in(name, sl(me, order), [bufs[3]]))

    def sum_phase(name, phase, half=None):
        _, g, sl, order, bufs = pieces[name]
        axis, done, buf = order[phase], order[:phase], bufs[phase]
        peers = [(k, moved(axis, k)) for k in (1, 2, 3)]
        if name[0] == "1" and axis == "z" and half != 0:
            copies = []
            both = half is None
            for k, co in peers:
                even = (z + k) % 2 == 0
                cond = jnp.logical_or(c0, even) if both else jnp.logical_and(c1, even)
                copies.append((cond, g.at[sl(co, done)], buf.at[k - 1], co))
            gone = [(jnp.logical_and(c1, zl == 0), buf.at[pl.ds(0, 1)]),
                    (jnp.logical_and(c1, zl == 1), buf.at[pl.ds(0, 2)])] + ([(c0, buf)] if both else [])
            return post(copies, [(real if both else jnp.logical_and(c1, zl == 0), buf)], gone)
        if name[0] == "1" and phase == 2 and half == 1:
            part = pl.ds(0, 512)
            copies = [(c1, g.at[sl(co, done, 512)], buf.at[k - 1, :, :, :, part], co) for k, co in peers]
            return post(copies, [(c1, buf.at[:, :, :, :, part])])
        cond = real if name[0] == "1" else None
        if half is not None:
            cond = c == half
        return post([(cond, g.at[sl(co, done)], buf.at[k - 1], co) for k, co in peers], [(cond, buf)])

    def add_phase(name, phase, batch, out=None):
        arrived(batch)
        _, _, sl, order, bufs = pieces[name]
        add_in(name, sl(me, order[:phase]), [bufs[phase].at[k] for k in range(3)], out)

    g5v = G5.reshape(2048, 640)

    def do_down_grad(n, carry):
        at = pl.ds(pl.multiple_of(n * 512, 512), 512)
        g5v[at, :] = mm_tn(HM[:, at], GD[...]).astype(BF)
        return carry
    lax.fori_loop(0, 4, do_down_grad, 0)
    s5 = sum_core("5")

    def do_ffn_back(n, carry):
        at = pl.ds(pl.multiple_of(n * 512, 512), 512)
        dh = mm_nt(GD[...], w5v[at, :])
        gate, up = GT[:, at].astype(F32), UT[:, at].astype(F32)
        k0, k1 = math.sqrt(2.0 / math.pi), 0.044715
        sq = gate * gate
        th = jnp.tanh(gate * (k0 + k0 * k1 * sq))
        half = 0.5 * (1.0 + th)
        slope = half + (0.5 * gate) * (1.0 - th * th) * (k0 + 3.0 * k0 * k1 * sq)
        dg = (dh * up * slope).astype(BF)
        du = (dh * (gate * half)).astype(BF)
        GT[:, at] = dg
        UT[:, at] = du
        G2[:, :, :, at] = mm(NFT[...], dg).astype(BF).reshape(4, 2, 80, 512)
        G3[:, :, :, at] = mm(NFT[...], du).astype(BF).reshape(4, 2, 80, 512)
        return carry
    lax.fori_loop(0, 2, do_ffn_back, 0)
    s2, s3 = sum_core("2", 0), sum_core("3", 0)
    add_core("5", s5)
    s5 = sum_phase("5", 2)
    lax.fori_loop(2, 3, do_ffn_back, 0)
    add_core("2", s2, 0)
    s2 = sum_phase("2", 2, 0)
    add_core("3", s3, 0)
    s3 = sum_phase("3", 2, 0)
    lax.fori_loop(3, 4, do_ffn_back, 0)
    t2, t3 = sum_core("2", 1), sum_core("3", 1)

    def do_ffn_in(n, carry):
        at = pl.ds(pl.multiple_of(n * 512, 512), 512)
        both = mm_nt(GT[:, at], cols_of(W2, n * 512, 512)) + mm_nt(UT[:, at], cols_of(W3, n * 512, 512))
        if carry is None:
            ACC[...] = both
        else:
            ACC[...] += both
        return carry
    do_ffn_in(0, None)
    add_core("2", t2, 1)
    s2 = s2 + sum_phase("2", 2, 1)
    add_core("3", t3, 1)
    s3 = s3 + sum_phase("3", 2, 1)
    lax.fori_loop(1, 4, do_ffn_in, 0)

    def do_mid(r):
        g = cv[r, :].astype(F32)
        dv, rowg = norm_back(HID[r, :], GV[4:5, :], ACC[r, :])
        GG[4:5, :] += jnp.sum(rowg, 0, keepdims=True)
        gh = g + dv
        HID[r, :] = gh
        db, rowo = norm_back(BR[r, :].astype(F32), GV[1:2, :], gh)
        GG[1:2, :] += jnp.sum(rowo, 0, keepdims=True)
        GD[r, :] = db.astype(BF)
    rows(128, do_mid)
    g4v = G4.reshape(1024, 768)

    for h in range(4):
        at = slice(256 * h, 256 * h + 256)
        g4v[at, 0:640] = mm(AMT[at, :], GD[...]).astype(BF)
        g4v[at, 640:768] = jnp.zeros((256, 128), BF)
        dam = mm_nt(GD[...], w4v[at, 0:640]).astype(BF)
        inner = jnp.sum(dam.astype(F32) * AM[:, at].astype(F32), -1, keepdims=True)
        for s in range(2):
            r = slice(256 * s, 256 * s + 256)
            DAM[s, h] = dam[r]
            DD[s, :, h:h + 1] = inner[r]
    s4 = sum_core("4")

    DKV[...] = jnp.zeros_like(DKV)
    for s in range(2):
        OA[...] = jnp.zeros_like(OA)

        def backward(kb, carry, s=s, progress={}):
            vis = seen(s, kb)
            keys, vals = KV[kb, :, 0:256], KV[kb, :, 256:512]
            dk = jnp.zeros((256, 256), F32)
            dv = jnp.zeros((256, 256), F32)
            for h in range(4):
                q, da = Q[s, h], DAM[s, h]
                p = jnp.where(vis, jnp.exp(mm_nt(q, keys)) * LI[s, :, h:h + 1], 0.0)
                ds = (p * (mm_nt(da, vals) - DD[s, :, h:h + 1])).astype(BF)
                OA[h] += mm(ds, keys)
                dk = dk + mm_tn(ds, q)
                dv = dv + mm_tn(p.astype(BF), da)
            DKV[kb, :, 0:256] += dk
            DKV[kb, :, 256:512] += dv
            for k, fn in progress.items():
                pl.when(kb == k)(fn)
            return carry
        held = {}

        def early():
            add_core("4", s4)
            held["4"] = sum_phase("4", 2)

        def one():
            add_phase("2", 2, s2)
            held["2"] = sum_phase("2", 1)

        steps = {0: early} if s == 0 else {2: one}
        lax.fori_loop(0, blocks[s] + 1, functools.partial(backward, progress=steps), 0)
        if s == 0:
            s4 = held["4"]
            add_phase("5", 2, s5)
            s5 = sum_phase("5", 1)
        else:
            s2 = held["2"]

        def query_back(h, carry, s=s):
            dq = turn_back(OA[h] * 0.0625, CS[s], SN[s])
            raw = QR[h, 256 * s:256 * s + 256, :].astype(F32)
            dv, rowg = norm_back(raw, GV[2:3, 0:256], dq)
            GG[2:3, 0:256] += jnp.sum(rowg, 0, keepdims=True)
            GT[256 * s:256 * s + 256, pl.ds(pl.multiple_of(h * 256, 256), 256)] = dv.astype(BF)
            return carry
        lax.fori_loop(0, 4, query_back, 0)
    for s in range(2):
        HM[256 * s:256 * s + 256, 0:512] = DKV[1 - c if s == 0 else 2 + c].astype(BF)
    dk_cp = send(HM.at[:, pl.ds(0, 512)], DKR, moved("c", 1))

    def do_qkv_grad(n, carry):
        at = pl.ds(pl.multiple_of(n * 512, 512), 512)
        W2[:, :, :, at] = mm(NRMT[...], GT[:, at]).astype(BF).reshape(4, 2, 80, 512)
        return carry
    lax.fori_loop(0, 2, do_qkv_grad, 0)
    s1 = sum_core("1", 0)
    add_phase("3", 2, s3)
    s3 = sum_phase("3", 1)
    arrived(dk_cp)
    for s in range(2):
        r = slice(256 * s, 256 * s + 256)
        tot = DKV[blocks[s]] + DKR[r, :].astype(F32)
        dk = turn_back(tot[:, 0:256], CS[s], SN[s])
        dv, rowg = norm_back(KR[r, :], GV[3:4, 0:256], dk)
        GG[3:4, 0:256] += jnp.sum(rowg, 0, keepdims=True)
        GT[r, 1024:1280] = dv.astype(BF)
        GT[r, 1280:1536] = tot[:, 256:512].astype(BF)
    do_qkv_grad(2, 0)
    t1 = sum_core("1", 1)
    add_core("1", s1, 0)
    s1a, s1b = sum_phase("1a", 2, 0), sum_phase("1b", 2, 0)

    def do_dnorm(n, carry):
        at = pl.ds(pl.multiple_of(n * 512, 512), 512)
        part = mm_nt(GT[:, at], w1_cols(n * 512, 512))
        if carry is None:
            ACC[...] = part
        else:
            ACC[...] += part
        return carry
    do_dnorm(0, None)
    add_core("1", t1, 1)
    s1a, s1b = s1a + sum_phase("1a", 2, 1), s1b + sum_phase("1b", 2, 1)
    add_phase("5", 1, s5)
    s5 = sum_phase("5", 0)
    lax.fori_loop(1, 3, do_dnorm, 0)
    add_phase("2", 1, s2)
    s2 = sum_phase("2", 0)
    add_phase("3", 1, s3)
    s3 = sum_phase("3", 0)
    all_gone(lo_sent)
    gxv = LO.reshape(T, D)

    def do_x(r):
        dv, rowg = norm_back(xv[r, :].astype(F32), GV[0:1, :], ACC[r, :])
        GG[0:1, :] += jnp.sum(rowg, 0, keepdims=True)
        gxv[r, :] = (HID[r, :] + dv).astype(BF)
    rows(128, do_x)
    gx_in = unshard(LO, o_gx)

    near = [dict(me, c=(c + dc) % 2, y=(y + dy) % 4) for dc in (0, 1) for dy in range(4) if dc + dy > 0]
    gs = post([(None, GG, GGR.at[i], co) for i, co in enumerate(near)], [(None, GGR.at[pl.ds(0, 7)])])

    def gain_step(axis, base, tot):
        GGR[base + 3] = tot
        return post(
            [(None, GGR.at[base + 3], GGR.at[base + k - 1], moved(axis, k)) for k in (1, 2, 3)],
            [(None, GGR.at[pl.ds(base, 3)])],
        )

    def gain_sum(lo, hi, tot):
        for k in range(lo, hi):
            tot = tot + GGR[k]
        return tot

    def into(k):
        def out(v):
            mf[k] = v.reshape(80, 128)
        return out

    def out_4(v):
        c4f[...] = v.reshape(16, 384)

    def out_down(v):
        MISC[0:16, :] = v.reshape(16, 640)

    add_phase("4", 2, s4)
    s4 = sum_phase("4", 1)
    add_phase("1b", 2, s1b)
    s1b = sum_phase("1b", 1)
    add_phase("1a", 2, s1a)
    s1a = sum_phase("1a", 1)
    arrived(gs)
    tot = gain_sum(0, 7, GG[...])
    gs = gain_step("z", 7, tot)
    add_phase("4", 1, s4)
    s4 = sum_phase("4", 0)
    add_phase("5", 0, s5, out_down)
    add_phase("2", 0, s2, into(1))
    add_phase("3", 0, s3, into(2))
    for e in range(16):
        for k in (1, 2):
            F2[e, 5 * k:5 * k + 5, :] = mf[k, 5 * e:5 * e + 5, :]
    add_phase("1b", 1, s1b)
    add_phase("1a", 1, s1a)
    s1 = sum_phase("1", 0)
    arrived(gs)
    tot = gain_sum(7, 10, tot)
    gs = gain_step("x", 11, tot)
    add_phase("4", 0, s4, out_4)
    pair = send(c4f.at[pl.ds(pl.multiple_of(8 * (1 - y % 2), 8), 8), :], R4, near_y())
    add_phase("1", 0, s1, into(0))
    for e in range(16):
        F2[e, 0:5, :] = mf[0, 5 * e:5 * e + 5, :]
    earlier = list(sent)
    sent.clear()
    home = post(
        [(None, F2.at[(j // 4) % 2 * 8 + j // 8 * 4 + j % 4], o_cols.at[gi], member(j)) for j in others],
        [(None, o_cols.at[pl.ds(0, 15)])],
    )
    keep_cols = pltpu.make_async_copy(F2.at[ge], o_cols.at[gi], ls)
    keep_cols.start()
    MISC[24:32, :] = jnp.zeros((8, D), F32)
    arrived(gs)
    tot = gain_sum(11, 14, tot)
    shard = f * 4 + y
    for k, (_, per, width) in enumerate(GAINS):
        line = tot[k:k + 1, 0:width]
        col = iota((1, width), 1)
        for r in range(per):
            MISC[24 + k:25 + k, r:r + 1] = jnp.sum(jnp.where(col == per * shard + r, line, 0.0), 1, keepdims=True)
    arrived(pair)
    own = c4f[pl.ds(pl.multiple_of(8 * (y % 2), 8), 8), :]
    left = y % 2 == 0
    MISC[16:24, 0:384] = jnp.where(left, own, R4[...])
    MISC[16:24, 384:640] = jnp.where(left, R4[...], own)[:, 0:256]
    keep_cols.wait()
    keep_rows = pltpu.make_async_copy(MISC, o_rows, ls)
    keep_rows.start()
    all_gone(earlier)
    keep_rows.wait()
    arrived(gx_in + lo_in + home)
    all_gone(sent)


def finish(lay, gx, cols, rows, o_layer, o_gx, o_q, o_k, o_v, o_o, o_gate, o_up, o_down, o0, o1, o2, o3, o4, o5):
    o_layer[...] = lay[...]
    for j in range(16):
        at = slice(128 * j, 128 * j + 128)
        v = cols[j]
        if j < 8:
            o_q[:, at] = v[0:5]
        elif j < 10:
            o_k[:, 128 * (j - 8):128 * (j - 7)] = v[0:5]
        elif j < 12:
            o_v[:, 128 * (j - 10):128 * (j - 9)] = v[0:5]
        o_gate[:, at] = v[5:10]
        o_up[:, at] = v[10:15]
    o_down[...] = rows[0:16, :]
    o_o[...] = rows[16:24, :]
    for k, ref in enumerate((o0, o1, o2, o3, o4, o5)):
        ref[...] = rows[24 + k:25 + k, 0:GAINS[k][1]]
    for m in range(2):
        o_gx[m] = gx[m].astype(F32)


def scratch():
    def v(*shape, dtype=F32):
        return pltpu.VMEM(shape, dtype)

    def b(*shape):
        return pltpu.VMEM(shape, BF)

    cols = (4, 2, 80, 2048)
    out = [
        b(*cols), b(*cols), b(*cols), b(4, 4, 2, 32, 768), b(4, 4, 2, 64, 640), b(4, 2, 16, 128),
        v(16, 16, 128), b(16, 16, 128), b(16, 16, 128), v(4, 80, 128), b(2, 16, 384), b(16, 384),
        v(2, 8, 128, dtype=I32),
        b(2, 256, D), b(2, 256, D), b(T, D), b(D, T), b(D, T), b(1024, T),
        v(2, 256, 128), v(2, 256, 128),
        v(2, 256, 1, dtype=I32), v(4, 1, 256, dtype=I32), v(8, D),
        b(4, T, 256), b(2, 4, 256, 256), v(T, 256), b(4, 256, 512), b(T, 1024),
        v(2, 256, 4), v(4, 256, 256), v(4, 256, 1),
        b(T, D), v(T, D), b(T, D), b(T, 2048), b(T, 2048), b(T, 2048), v(T, D), b(T, D),
        b(2, 256, D),
        b(2, 4, 256, 256), v(2, 256, 4), v(4, 256, 512), b(T, 512),
        b(*cols), b(*cols), b(4, 4, 2, 32, 768), b(4, 4, 2, 64, 640),
        b(4, 2, 80, 1024), b(4, 2, 80, 1024), b(4, 2, 80, 1024), b(4, 4, 1, 32, 768), b(4, 4, 1, 64, 640),
        b(3, 1, 2, 48, 1024), b(3, 4, 1, 32, 512), b(3, 1, 2, 80, 1024), b(3, 4, 1, 80, 512),
        b(3, 4, 4, 1, 16, 384), b(3, 4, 4, 1, 16, 640),
        b(3, 1, 1, 48, 512), b(3, 1, 1, 32, 512), b(3, 1, 1, 80, 512), b(3, 1, 1, 80, 512),
        b(3, 1, 4, 1, 16, 384), b(3, 4, 1, 1, 16, 640),
        b(3, 1, 1, 80, 128), b(3, 1, 1, 80, 128), b(3, 1, 1, 80, 128), b(3, 1, 1, 1, 16, 384), b(3, 1, 1, 1, 16, 640),
        v(8, D), v(15, 8, D), v(16, 16, 128), v(16, 384), v(8, 384), v(32, D),
        pltpu.SemaphoreType.DMA((N_SEM,)), pltpu.SemaphoreType.DMA((N_SEM,)), pltpu.SemaphoreType.DMA,
    ]
    return out


def on_device(tokens_in, cotangent, doc_lengths, w_query, w_key, w_value, w_out, gain_attn_in, gain_attn_out,
              gain_query, gain_key, w_gate, w_up, w_down, gain_ffn_in, gain_ffn_out):
    gains = [g.reshape(1, -1) for g in (gain_attn_in, gain_attn_out, gain_query, gain_key, gain_ffn_in, gain_ffn_out)]
    vm = pl.BlockSpec(memory_space=pltpu.VMEM)
    hbm = pl.BlockSpec(memory_space=pl.ANY)

    def s(*shape, dtype=F32):
        return jax.ShapeDtypeStruct(shape, dtype)

    parts = pl.pallas_call(
        kernel,
        out_shape=(s(2, 256, D, dtype=BF), s(2, 256, D, dtype=BF), s(16, 16, 128), s(32, D)),
        in_specs=[hbm, hbm] + [vm] * 14,
        out_specs=(hbm,) * 4,
        scratch_shapes=scratch(),
        compiler_params=pltpu.CompilerParams(
            collective_id=0, has_side_effects=True, vmem_limit_bytes=64 * 1024 * 1024 - 65536
        ),
        name="block",
    )(tokens_in, cotangent, doc_lengths, *gains, w_query, w_key, w_value, w_out, w_gate, w_up, w_down)
    outs = pl.pallas_call(
        finish,
        out_shape=(
            s(2, 256, D, dtype=BF), s(2, 256, D), s(5, 1024), s(5, 256), s(5, 256), s(8, D), s(5, 2048), s(5, 2048),
            s(16, D), s(1, 5), s(1, 5), s(1, 2), s(1, 2), s(1, 5), s(1, 5),
        ),
        in_specs=[vm] * 4,
        out_specs=(vm,) * 15,
        name="finish",
    )(*parts)
    (layer_out, grad_x, gq, gk, gv, go, ggate, gup, gdown, g0, g1, g2, g3, g4, g5) = outs
    return (
        layer_out, grad_x, gq, gk, gv, go, g0.reshape(-1), g1.reshape(-1), g2.reshape(-1), g3.reshape(-1),
        ggate, gup, gdown, g4.reshape(-1), g5.reshape(-1),
    )


def solution(mesh):
    both = ("fsdp", "dp")
    row, gain = P(both, None), P(both)
    tok = P(None, both, None)
    return jax.shard_map(
        on_device,
        mesh=mesh,
        in_specs=(tok, tok, P("fsdp", None, None), row, row, row, row, gain, gain, gain, gain, row, row, row, gain, gain),
        out_specs=(tok, tok, row, row, row, row, gain, gain, gain, gain, row, row, row, gain, gain),
        check_vma=False,
    )
```

```python
import functools
import math

import jax
import jax.numpy as jnp
from jax import lax
from jax.experimental import pallas as pl
from jax.experimental.pallas import tpu as pltpu
from jax.sharding import PartitionSpec as P

MESH = pl.DeviceIdType.MESH
F32 = jnp.float32
BF = jnp.bfloat16
I32 = jnp.int32
EPS = 1e-06
THETA = 1000000.0
T = 512
D = 640
GAINS = ((0, 5, 640), (5, 5, 640), (10, 2, 256), (12, 2, 256), (14, 5, 640), (19, 5, 640))
N_SEM = 96


def mm(a, b):
    return lax.dot_general(a, b, (((1,), (0,)), ((), ())), preferred_element_type=F32)


def mm_nt(a, b):
    return lax.dot_general(a, b, (((1,), (1,)), ((), ())), preferred_element_type=F32)


def mm_tn(a, b):
    return lax.dot_general(a, b, (((0,), (0,)), ((), ())), preferred_element_type=F32)


def mean_last(v):
    return jnp.mean(v, -1, keepdims=True)


def inv_rms(v):
    return lax.rsqrt(mean_last(v * v) + EPS)


def iota(shape, dim):
    return lax.broadcasted_iota(I32, shape, dim)


def norm_back(v, gain, grad):
    r = inv_rms(v)
    hat = v * r
    gg = grad * gain
    return r * (gg - hat * mean_last(gg * hat)), grad * hat


def kernel(
    tok, cot, dl, n0, n1, n2, n3, n4, n5, wq, wk, wv, wo, wg, wu, wd,
    o_layer, o_gx, o_cols, o_rows,
    W1, W2, W3, W4, W5, GW, stf, stage, R1, mf, po, PR, DLB,
    XB, CB, NRM, NRMT, NFT, AMT, CS, SN, DCOL, DROW, GV, QR, Q, KR, KV, AM, LI, OA, LA, BR, HID, NF, GT, UT, HM, ACC, GD, LO,
    DAM, DD, DKV, DKR,
    G2, G3, G4, G5, C1, C2, C3, C4, C5, A1a, A1b, A2, A3, A4, A5, B1a, B1b, B2, B3, B4, B5,
    E1, E2, E3, E4, E5, GG, GGR, F2, c4f, R4, MISC, ss, rs, ls,
):
    f = lax.axis_index("fsdp")
    y = lax.axis_index("dp")
    x = f // 8
    z = (f // 2) % 4
    c = f % 2
    zh, zl = z // 2, z % 2
    me = {"x": x, "z": z, "c": c, "y": y}
    gi = c * 8 + zl * 4 + y
    ge = zl * 8 + c * 4 + y

    def dev(co):
        return ((co["x"] * 4 + co["z"]) * 2 + co["c"], co["y"])

    def member(j):
        return {"x": x, "z": zh * 2 + (j // 4) % 2, "c": j // 8, "y": j % 4}

    def moved(axis, k):
        co = dict(me)
        co[axis] = (me[axis] + k) % (2 if axis == "c" else 4)
        return co

    def near_y():
        return dict(me, y=y + 1 - 2 * (y % 2))

    def under(cond, fn):
        if cond is None:
            fn()
        else:
            pl.when(cond)(fn)

    count = [0]

    def fresh():
        count[0] += 1
        assert count[0] <= N_SEM
        return count[0] - 1

    sent = []

    def remote(src, dst, i, co):
        return pltpu.make_async_remote_copy(
            src_ref=src, dst_ref=dst, send_sem=ss.at[i], recv_sem=rs.at[i], device_id=dev(co), device_id_type=MESH
        )

    def post(copies, come, gone=None):
        i = fresh()
        for cond, src, dst, co in copies:
            under(cond, lambda src=src, dst=dst, co=co: remote(src, dst, i, co).start())
        sent.append((i, come if gone is None else gone))
        return [(i, come)]

    def send(src, dst, co):
        return post([(None, src, dst, co)], [(None, dst)])

    def arrived(batches):
        for i, come in batches:
            for cond, ref in come:
                under(cond, lambda i=i, ref=ref: remote(ref, ref, i, moved("c", 1)).wait_recv())

    def all_gone(batches):
        for i, gone in batches:
            for cond, ref in gone:
                under(cond, lambda i=i, ref=ref: remote(ref, ref, i, moved("c", 1)).wait_send())
        batches.clear()

    def sl_cols(r0, rn):
        def sl(co, done, width=1024):
            xs = slice(None) if "x" in done else pl.ds(co["x"], 1)
            zs = slice(None) if "z" in done else pl.ds(co["z"] // 2, 1)
            if "y" not in done:
                cs, w = co["c"] * 1024 + (co["z"] % 2) * 512 + co["y"] * 128, 128
            elif "z" not in done:
                cs, w = co["c"] * 1024 + (co["z"] % 2) * 512, 512
            else:
                cs, w = co["c"] * 1024, width
            return (xs, zs, pl.ds(r0, rn), pl.ds(pl.multiple_of(cs, 128), w))
        return sl

    def sl_out(co, done):
        xs = slice(None) if "x" in done else pl.ds(co["x"], 1)
        zs = slice(None) if "z" in done else pl.ds(co["z"], 1)
        if "y" in done:
            return (xs, zs, pl.ds(co["c"], 1), pl.ds(0, 32), pl.ds(0, 768))
        return (
            xs, zs, pl.ds(co["c"], 1),
            pl.ds(pl.multiple_of((co["y"] // 2) * 16, 16), 16), pl.ds(pl.multiple_of((co["y"] % 2) * 384, 128), 384),
        )

    def sl_down(co, done):
        xs = slice(None) if "x" in done else pl.ds(co["x"], 1)
        zs = slice(None) if "z" in done else pl.ds(co["z"], 1)
        rows = pl.ds(0, 64) if "y" in done else pl.ds(pl.multiple_of(co["y"] * 16, 16), 16)
        return (xs, zs, pl.ds(co["c"], 1), rows, pl.ds(0, 640))

    pieces = {
        "1": (W1, W2, sl_cols(0, 80), "yzx", (E1, None, None, C1)),
        "1a": (W1, W2, sl_cols(0, 48), "yzx", (None, B1a, A1a, None)),
        "1b": (W1, W2, sl_cols(48, 32), "yxz", (None, B1b, A1b, None)),
        "2": (W2, G2, sl_cols(0, 80), "yzx", (E2, B2, A2, C2)),
        "3": (W3, G3, sl_cols(0, 80), "yxz", (E3, B3, A3, C3)),
        "4": (W4, G4, sl_out, "zxy", (E4, B4, A4, C4)),
        "5": (W5, G5, sl_down, "xzy", (E5, B5, A5, C5)),
    }
    real = jnp.logical_or(c == 0, zl == 0)
    c0, c1 = c == 0, c == 1

    def gather(name, phase):
        w, _, sl, order, bufs = pieces[name]
        done = order[:phase]
        if name[0] == "1" and phase >= 2:
            wide, half = w.at[sl(me, done)], w.at[sl(me, done, 512)]
            if phase == 3:
                to = moved("c", 1)
                return post([(c0, wide, wide, to), (c1, half, half, to)], [(c0, half), (c1, wide)], [(c0, wide), (c1, half)])
            if order[2] == "z":
                ref = w.at[sl(me, done)]
                return post1z(name, phase, ref)
            to = [moved(order[phase], k) for k in (1, 2, 3)]
            b = bufs[phase]
            come = [(c0, b), (c1, b.at[:, :, :, :, pl.ds(0, 512)])]
            return post([(c0, wide, wide, t) for t in to] + [(c1, half, half, t) for t in to], come)
        ref = w.at[sl(me, done)]
        if phase == 3:
            return send(ref, ref, moved("c", 1))
        if name[0] == "1" and order[phase] == "z":
            return post1z(name, phase, ref)
        cond = real if name[0] == "1" else None
        copies = [(cond, ref, ref, moved(order[phase], k)) for k in (1, 2, 3)]
        return post(copies, [(cond, bufs[phase])])

    def ring(name, step):
        w, _, sl, order, bufs = pieces[name]
        axis, done, buf = order[2], order[:2], bufs[2]
        right, left = moved(axis, 1), moved(axis, 3)
        if step == 0:
            ref = w.at[sl(me, done)]
            return post([(None, ref, ref, right), (None, ref, ref, left)], [(None, buf.at[pl.ds(0, 2)])])

        def half(co, k):
            at = sl(co, done)
            n = at[3].size // 2
            return w.at[at[:3] + (pl.ds(pl.multiple_of(at[3].start + k * n, 128), n),)]
        one, two = half(left, 0), half(right, 1)
        return post([(None, one, one, right), (None, two, two, left)], [(None, buf.at[pl.ds(0, 1)])])

    def post1z(name, phase, ref):
        b = pieces[name][4][phase]
        come = [
            (c0, b), (jnp.logical_and(c1, zl == 0), b.at[pl.ds(0, 1)]), (jnp.logical_and(c1, zl == 1), b.at[pl.ds(0, 2)]),
        ]
        return post([(real, ref, ref, moved("z", k)) for k in (1, 2, 3)], come, [(real, b)])

    bar = pltpu.get_barrier_semaphore()
    friends = [member((gi + d) % 16) for d in range(1, 16)]
    friends += [moved("z", 2)] + [dict(me, z=(zh * 2 + 2) % 4 + (1 - zl))] + [moved("x", k) for k in (1, 2, 3)]
    for co in friends:
        pl.semaphore_signal(bar, inc=1, device_id=dev(co), device_id_type=MESH)

    lane = iota((1, 128), 1)
    grow = jnp.zeros((1, 128), F32)
    for ref, (at, per, _) in zip((n0, n1, n2, n3, n4, n5), GAINS):
        own = ref[...].astype(F32)
        for r in range(per):
            grow = jnp.where(lane == at + r, own[0:1, r:r + 1], grow)
    for j in range(16):
        cols = slice(128 * j, 128 * j + 128)
        if j < 8:
            part = wq[:, cols]
        elif j < 10:
            part = wk[:, 128 * (j - 8):128 * (j - 7)]
        elif j < 12:
            part = wv[:, 128 * (j - 10):128 * (j - 9)]
        else:
            part = None
        stf[j, 0:5, :] = jnp.zeros((5, 128), F32) if part is None else part.astype(F32)
        stf[j, 5:10, :] = wg[:, cols].astype(F32)
        stf[j, 10:15, :] = wu[:, cols].astype(F32)
        stf[j, 15:16, :] = grow
    stage[...] = stf[...].astype(BF)
    wof = wo[...].astype(F32)
    twice = jnp.concatenate([wof, wof], axis=0)
    keep = (iota((16, 640), 0) // 8) == (y % 2)
    twice = jnp.where(keep, twice, 0.0).astype(BF)
    po[0, :, :] = twice[:, 0:384]
    po[1, :, 0:256] = twice[:, 384:640]
    po[1, :, 256:384] = jnp.zeros((16, 128), BF)
    rowid = iota((8, 128), 0)
    tile = jnp.zeros((8, 128), I32)
    for k in range(6):
        tile = jnp.where(rowid == k, dl[0, k // 3:k // 3 + 1, k % 3:k % 3 + 1], tile)
    DLB[c] = tile
    W5[x, z, c, pl.ds(pl.multiple_of(y * 16, 16), 16), :] = wd[...]

    pl.semaphore_wait(bar, len(friends))

    core_to = ((y + 1) // 2) % 2
    blocks = (c, 3 - c)
    micro = y // 2

    def either(v, fn):
        for k in (0, 1):
            pl.when(v == k)(lambda k=k: fn(k))

    def reorder(src, dst, to, mine_in, slot_of):
        i = (fresh(), fresh())
        away = []
        for k in (0, 1):
            own = jnp.logical_and(to[k]["c"] == c, to[k]["y"] == y)
            far = jnp.logical_not(own)

            def start_far(s, k=k):
                pltpu.make_async_remote_copy(
                    src_ref=src.at[k], dst_ref=dst.at[s], send_sem=ss.at[i[k]], recv_sem=rs.at[i[s]],
                    device_id=dev(to[k]), device_id_type=MESH,
                ).start()

            def copy_own(s, k=k):
                cp = pltpu.make_async_copy(src.at[k], dst.at[s], ls)
                cp.start()
                cp.wait()

            for s in (0, 1):
                pl.when(jnp.logical_and(far, slot_of[k] == s))(lambda s=s, f=start_far: f(s))
            for s in (0, 1):
                pl.when(jnp.logical_and(own, slot_of[k] == s))(lambda s=s, f=copy_own: f(s))
            away.append((i[k], [(far, src.at[k])]))
        sent.extend(away)
        return [(i[k], [(jnp.logical_not(mine_in[k]), dst.at[k])]) for k in (0, 1)]

    def reshard(src, dst):
        to = [dict(me, c=core_to, y=c + 2 * m) for m in (0, 1)]
        mine = [jnp.logical_and(blocks[s] == y, c == y % 2) for s in (0, 1)]
        return reorder(src, dst, to, mine, (micro, micro))

    def unshard(src, dst):
        to = [dict(me, c=y % 2, y=blocks[s]) for s in (0, 1)]
        mine = [jnp.logical_and(core_to == c, y == c + 2 * m) for m in (0, 1)]
        return reorder(src, dst, to, mine, (micro, micro))

    others = [(gi + d) % 16 for d in range(1, 16)]
    a2a = post([(None, stage.at[j], R1.at[ge], member(j)) for j in others], [(None, R1.at[pl.ds(0, 15)])])
    R1[ge] = stage[gi]
    pair = send(po.at[1 - y % 2], PR, near_y())
    lens_cp = send(DLB.at[c], DLB.at[c], moved("c", 1))
    g5 = gather("5", 0)

    arrived(a2a)
    for e in range(16):
        v = R1[e].astype(F32)
        for k in range(3):
            mf[k, 5 * e:5 * e + 5, :] = v[5 * k:5 * k + 5, :]
        mf[3, e:e + 1, :] = v[15:16, :]
    own_cols = pl.ds(pl.multiple_of(c * 1024 + zl * 512 + y * 128, 128), 128)
    W1[x, zh, :, own_cols] = mf[0].astype(BF)
    g1 = gather("1", 0)
    GW[x, zh] = mf[3, 0:16, :].astype(BF)
    gz = send(GW.at[x, zh], GW.at[x, zh], moved("z", 2))
    for w, k in ((W2, 1), (W3, 2)):
        w[x, zh, :, own_cols] = mf[k].astype(BF)
    arrived(pair)
    W4[x, z, c, pl.ds(pl.multiple_of((y // 2) * 16, 16), 16), pl.ds(pl.multiple_of((y % 2) * 384, 128), 384)] = (
        po[y % 2].astype(F32) + PR[...].astype(F32)
    ).astype(BF)
    g4, g2, g3 = gather("4", 0), gather("2", 0), gather("3", 0)
    arrived(g1)
    g1a, g1b = gather("1a", 1), gather("1b", 1)
    x_in = reshard(tok, XB)
    arrived(gz)
    gx = post([(None, GW.at[x], GW.at[x], moved("x", k)) for k in (1, 2, 3)], [(None, GW.at[pl.ds(0, 3)])])
    arrived(g1a)
    g1a = gather("1a", 2)
    arrived(g1b)
    g1b = gather("1b", 2)
    arrived(g4)
    g4 = gather("4", 1)
    arrived(g2)
    g2 = gather("2", 1)
    arrived(g3)
    g3 = gather("3", 1)
    arrived(g5)
    g5 = gather("5", 1)

    def doc_rows():
        lt = DLB[y % 2]
        first = y // 2 == 0
        l0 = jnp.where(first, lt[0:1, :], lt[3:4, :])[:, 0:1]
        l1 = jnp.where(first, lt[1:2, :], lt[4:5, :])[:, 0:1]
        return l0, l0, l1, l0 + l1

    def angles(s):
        l0, e0, l1, e1 = doc_rows()
        freq = jnp.exp(iota((1, 128), 1).astype(F32) * (-2.0 * math.log(THETA) / 256))
        t = blocks[s] * 256 + iota((256, 1), 0)
        p0, p1 = (t >= e0).astype(I32), (t >= e1).astype(I32)
        DCOL[s] = p0 + p1
        turned = (t - p0 * l0 - p1 * l1).astype(F32) * freq
        CS[s] = jnp.cos(turned)
        SN[s] = jnp.sin(turned)

    arrived(lens_cp)
    l0, e0, l1, e1 = doc_rows()
    for k in range(4):
        t = 256 * k + iota((1, 256), 1)
        DROW[k] = (t >= e0).astype(I32) + (t >= e1).astype(I32)
    angles(0)
    angles(1)
    arrived(gx)

    packed = GW[...].reshape(128, 128)
    for k, (lane, per, width) in enumerate(GAINS):
        col = iota((128, width), 1)
        shard = iota((128, width), 0)
        colf = col.astype(F32)
        rest = colf - per * jnp.floor((colf + 0.5) * (1.0 / per))
        pick = jnp.where(shard.astype(F32) == rest + lane, 1.0, 0.0).astype(BF)
        spread = mm(packed, pick)
        mine = jnp.logical_and(col >= per * shard, col < per * shard + per)
        GV[k:k + 1, 0:width] = jnp.sum(jnp.where(mine, spread, 0.0), 0, keepdims=True)

    def rows(n, fn):
        def step(i, carry):
            fn(pl.ds(pl.multiple_of(i * n, n), n))
            return carry
        lax.fori_loop(0, T // n, step, 0)

    xv = XB.reshape(T, D)
    cv = CB.reshape(T, D)
    csv, snv = CS.reshape(T, 128), SN.reshape(T, 128)

    def do_norm(r):
        v = xv[r, :].astype(F32)
        NRM[r, :] = (v * inv_rms(v) * GV[0:1, :]).astype(BF)
    arrived(x_in)
    rows(128, do_norm)
    arrived(g4)
    g4 = gather("4", 2)
    arrived(g1a + g1b)
    g1 = gather("1", 3)
    arrived(g2)
    g2 = ring("2", 0)
    arrived(g3)
    g3 = ring("3", 0)
    arrived(g5)
    g5 = gather("5", 2)
    NRMT[...] = NRM[...].T
    arrived(g1)

    def w1_cols(start, width):
        return W1[:, :, :, pl.ds(pl.multiple_of(start, 128), width)].reshape(D, width)

    def turn(u, cs, sn):
        u1, u2 = u[:, 0:128], u[:, 128:256]
        return u1 * cs - u2 * sn, u2 * cs + u1 * sn

    def turn_back(u, cs, sn):
        u1, u2 = u[:, 0:128], u[:, 128:256]
        return jnp.concatenate([u1 * cs + u2 * sn, u2 * cs - u1 * sn], -1)

    raw = mm(NRM[...], w1_cols(1024, 256))
    KR[...] = raw
    o1, o2 = turn(raw * inv_rms(raw) * GV[3:4, 0:256], csv[...], snv[...])
    vals = mm(NRM[...], w1_cols(1280, 256))
    for s in range(2):
        r = slice(256 * s, 256 * s + 256)
        KV[blocks[s], :, 0:128] = o1[r].astype(BF)
        KV[blocks[s], :, 128:256] = o2[r].astype(BF)
        KV[blocks[s], :, 256:512] = vals[r].astype(BF)
    kv_cp = sum([send(KV.at[blocks[s]], KV.at[blocks[s]], moved("c", 1)) for s in range(2)], [])

    def do_query(h, carry):
        raw = mm(NRM[...], w1_cols(h * 256, 256))
        QR[h] = raw.astype(BF)
        o1, o2 = turn(raw * inv_rms(raw) * GV[2:3, 0:256], csv[...], snv[...])
        for s in range(2):
            r = slice(256 * s, 256 * s + 256)
            Q[s, h, :, 0:128] = (o1[r] * 0.0625).astype(BF)
            Q[s, h, :, 128:256] = (o2[r] * 0.0625).astype(BF)
        return carry
    lax.fori_loop(0, 4, do_query, 0)

    arrived(kv_cp)

    def seen(s, kb):
        t = blocks[s] * 256 + iota((256, 256), 0)
        k = kb * 256 + iota((256, 256), 1)
        return jnp.logical_and(DCOL[s] == DROW[kb], t >= k)

    for s in range(2):
        OA[...] = jnp.zeros_like(OA)
        LA[...] = jnp.zeros_like(LA)

        def forward(kb, carry, s=s, progress={}):
            vis = seen(s, kb)
            keys, vals = KV[kb, :, 0:256], KV[kb, :, 256:512]
            for h in range(4):
                p = jnp.where(vis, jnp.exp(mm_nt(Q[s, h], keys)), 0.0)
                LA[h] += jnp.sum(p, -1, keepdims=True)
                OA[h] += mm(p.astype(BF), vals)
            for k, fn in progress.items():
                pl.when(kb == k)(fn)
            return carry
        held = {}

        def core_four():
            arrived(g4)
            held["4"] = gather("4", 3)

        def pass_on():
            arrived(g2 + g3)
            held["2"], held["3"] = ring("2", 1), ring("3", 1)

        steps = {} if s == 0 else {1: core_four, 2: pass_on}
        lax.fori_loop(0, blocks[s] + 1, functools.partial(forward, progress=steps), 0)
        for h in range(4):
            inv = 1.0 / LA[h]
            LI[s, :, h:h + 1] = inv
            mixed = (OA[h] * inv).astype(BF)
            AM[256 * s:256 * s + 256, 256 * h:256 * h + 256] = mixed
            AMT[256 * h:256 * h + 256, 256 * s:256 * s + 256] = mixed.T
    g4, g2, g3 = held["4"], held["2"], held["3"]
    c_in = reshard(cot, CB)
    arrived(g2 + g3)
    g2, g3 = gather("2", 3), gather("3", 3)
    arrived(g4)
    w4v = W4.reshape(1024, 768)
    w5v = W5.reshape(2048, 640)

    def do_out(r):
        b = mm(AM[r, :], w4v[:, 0:640])
        BR[r, :] = b.astype(BF)
        hid = xv[r, :].astype(F32) + b * inv_rms(b) * GV[1:2, :]
        HID[r, :] = hid
        NF[r, :] = (hid * inv_rms(hid) * GV[4:5, :]).astype(BF)
    rows(256, do_out)
    NFT[...] = NF[...].T
    arrived(g2 + g3)

    def cols_of(w, at, width):
        return w[:, :, :, pl.ds(pl.multiple_of(at, 128), width)].reshape(D, width)

    def do_ffn(n, carry):
        at = pl.ds(pl.multiple_of(n * 512, 512), 512)
        gate = mm(NF[...], cols_of(W2, n * 512, 512))
        up = mm(NF[...], cols_of(W3, n * 512, 512))
        GT[:, at] = gate.astype(BF)
        UT[:, at] = up.astype(BF)
        HM[:, at] = (jax.nn.gelu(gate, approximate=True) * up).astype(BF)
        return carry
    lax.fori_loop(0, 2, do_ffn, 0)
    arrived(g5)
    g5 = gather("5", 3)
    lax.fori_loop(2, 4, do_ffn, 0)
    arrived(g5)

    arrived(c_in)
    all_gone(sent)
    GG[...] = jnp.zeros_like(GG)
    lov = LO.reshape(T, D)

    def do_down(r):
        d = mm(HM[r, :], w5v[...])
        rd = inv_rms(d)
        hat = d * rd
        lov[r, :] = (HID[r, :] + hat * GV[5:6, :]).astype(BF)
        g = cv[r, :].astype(F32)
        gg = g * GV[5:6, :]
        GD[r, :] = (rd * (gg - hat * mean_last(gg * hat))).astype(BF)
        GG[5:6, :] += jnp.sum(g * hat, 0, keepdims=True)
    rows(256, do_down)
    lo_in = unshard(LO, o_layer)
    lo_sent = list(sent)
    sent.clear()

    def sum_core(name, half=None):
        _, g, sl, order, bufs = pieces[name]
        to, buf = moved("c", 1), bufs[3]
        if half == 0:
            return post([(c1, g.at[sl(to, order)], buf, to)], [(c0, buf)], [(c1, buf)])
        if half == 1:
            wide = 512 if name == "1" else 1024
            buf = buf.at[:, :, :, pl.ds(0, wide)]
            return post([(c0, g.at[sl(to, order, wide)], buf, to)], [(c1, buf)], [(c0, buf)])
        return send(g.at[sl(to, order)], buf, to)

    def add_in(name, idx, bufs, out=None):
        g = pieces[name][1]
        shape = bufs[0].shape
        n1 = shape[1]
        kind = BF if len(bufs) == 1 else F32

        def at(s, k):
            return pl.ds(k if s == slice(None) else s.start + k, 1)

        def step(i, carry):
            here = (at(idx[0], i // n1), at(idx[1], i % n1)) + tuple(idx[2:])
            tot = g[here].astype(kind)
            for b in bufs:
                tot = tot + b[pl.ds(i // n1, 1), pl.ds(i % n1, 1)].astype(kind)
            if out is None:
                g[here] = tot.astype(BF)
            else:
                out(tot)
            return carry
        if shape[0] * n1 == 1:
            step(0, 0)
        else:
            lax.fori_loop(0, shape[0] * n1, step, 0)

    def add_core(name, batch, half=None):
        arrived(batch)
        _, _, sl, order, bufs = pieces[name]
        under(None if half is None else c == half, lambda: add_in(name, sl(me, order), [bufs[3]]))

    def sum_phase(name, phase, half=None):
        _, g, sl, order, bufs = pieces[name]
        axis, done, buf = order[phase], order[:phase], bufs[phase]
        peers = [(k, moved(axis, k)) for k in (1, 2, 3)]
        if name[0] == "1" and axis == "z" and half != 0:
            copies = []
            both = half is None
            for k, co in peers:
                even = (z + k) % 2 == 0
                cond = jnp.logical_or(c0, even) if both else jnp.logical_and(c1, even)
                copies.append((cond, g.at[sl(co, done)], buf.at[k - 1], co))
            gone = [(jnp.logical_and(c1, zl == 0), buf.at[pl.ds(0, 1)]),
                    (jnp.logical_and(c1, zl == 1), buf.at[pl.ds(0, 2)])] + ([(c0, buf)] if both else [])
            return post(copies, [(real if both else jnp.logical_and(c1, zl == 0), buf)], gone)
        if name[0] == "1" and phase == 2 and half == 1:
            part = pl.ds(0, 512)
            copies = [(c1, g.at[sl(co, done, 512)], buf.at[k - 1, :, :, :, part], co) for k, co in peers]
            return post(copies, [(c1, buf.at[:, :, :, :, part])])
        cond = real if name[0] == "1" else None
        if half is not None:
            cond = c == half
        return post([(cond, g.at[sl(co, done)], buf.at[k - 1], co) for k, co in peers], [(cond, buf)])

    def add_phase(name, phase, batch, out=None):
        arrived(batch)
        _, _, sl, order, bufs = pieces[name]
        add_in(name, sl(me, order[:phase]), [bufs[phase].at[k] for k in range(3)], out)

    g5v = G5.reshape(2048, 640)

    def do_down_grad(n, carry):
        at = pl.ds(pl.multiple_of(n * 512, 512), 512)
        g5v[at, :] = mm_tn(HM[:, at], GD[...]).astype(BF)
        return carry
    lax.fori_loop(0, 4, do_down_grad, 0)
    s5 = sum_core("5")

    def do_ffn_back(n, carry):
        at = pl.ds(pl.multiple_of(n * 512, 512), 512)
        dh = mm_nt(GD[...], w5v[at, :])
        gate, up = GT[:, at].astype(F32), UT[:, at].astype(F32)
        k0, k1 = math.sqrt(2.0 / math.pi), 0.044715
        sq = gate * gate
        th = jnp.tanh(gate * (k0 + k0 * k1 * sq))
        half = 0.5 * (1.0 + th)
        slope = half + (0.5 * gate) * (1.0 - th * th) * (k0 + 3.0 * k0 * k1 * sq)
        dg = (dh * up * slope).astype(BF)
        du = (dh * (gate * half)).astype(BF)
        GT[:, at] = dg
        UT[:, at] = du
        G2[:, :, :, at] = mm(NFT[...], dg).astype(BF).reshape(4, 2, 80, 512)
        G3[:, :, :, at] = mm(NFT[...], du).astype(BF).reshape(4, 2, 80, 512)
        return carry
    lax.fori_loop(0, 2, do_ffn_back, 0)
    s2, s3 = sum_core("2", 0), sum_core("3", 0)
    add_core("5", s5)
    s5 = sum_phase("5", 2)
    lax.fori_loop(2, 3, do_ffn_back, 0)
    add_core("2", s2, 0)
    s2 = sum_phase("2", 2, 0)
    add_core("3", s3, 0)
    s3 = sum_phase("3", 2, 0)
    lax.fori_loop(3, 4, do_ffn_back, 0)
    t2, t3 = sum_core("2", 1), sum_core("3", 1)

    def do_ffn_in(n, carry):
        at = pl.ds(pl.multiple_of(n * 512, 512), 512)
        both = mm_nt(GT[:, at], cols_of(W2, n * 512, 512)) + mm_nt(UT[:, at], cols_of(W3, n * 512, 512))
        if carry is None:
            ACC[...] = both
        else:
            ACC[...] += both
        return carry
    do_ffn_in(0, None)
    add_core("2", t2, 1)
    s2 = s2 + sum_phase("2", 2, 1)
    add_core("3", t3, 1)
    s3 = s3 + sum_phase("3", 2, 1)
    lax.fori_loop(1, 4, do_ffn_in, 0)

    def do_mid(r):
        g = cv[r, :].astype(F32)
        dv, rowg = norm_back(HID[r, :], GV[4:5, :], ACC[r, :])
        GG[4:5, :] += jnp.sum(rowg, 0, keepdims=True)
        gh = g + dv
        HID[r, :] = gh
        db, rowo = norm_back(BR[r, :].astype(F32), GV[1:2, :], gh)
        GG[1:2, :] += jnp.sum(rowo, 0, keepdims=True)
        GD[r, :] = db.astype(BF)
    rows(128, do_mid)
    g4v = G4.reshape(1024, 768)

    for h in range(4):
        at = slice(256 * h, 256 * h + 256)
        g4v[at, 0:640] = mm(AMT[at, :], GD[...]).astype(BF)
        g4v[at, 640:768] = jnp.zeros((256, 128), BF)
        dam = mm_nt(GD[...], w4v[at, 0:640]).astype(BF)
        inner = jnp.sum(dam.astype(F32) * AM[:, at].astype(F32), -1, keepdims=True)
        for s in range(2):
            r = slice(256 * s, 256 * s + 256)
            DAM[s, h] = dam[r]
            DD[s, :, h:h + 1] = inner[r]
    s4 = sum_core("4")

    DKV[...] = jnp.zeros_like(DKV)
    for s in range(2):
        OA[...] = jnp.zeros_like(OA)

        def backward(kb, carry, s=s, progress={}):
            vis = seen(s, kb)
            keys, vals = KV[kb, :, 0:256], KV[kb, :, 256:512]
            dk = jnp.zeros((256, 256), F32)
            dv = jnp.zeros((256, 256), F32)
            for h in range(4):
                q, da = Q[s, h], DAM[s, h]
                p = jnp.where(vis, jnp.exp(mm_nt(q, keys)) * LI[s, :, h:h + 1], 0.0)
                ds = (p * (mm_nt(da, vals) - DD[s, :, h:h + 1])).astype(BF)
                OA[h] += mm(ds, keys)
                dk = dk + mm_tn(ds, q)
                dv = dv + mm_tn(p.astype(BF), da)
            DKV[kb, :, 0:256] += dk
            DKV[kb, :, 256:512] += dv
            for k, fn in progress.items():
                pl.when(kb == k)(fn)
            return carry
        held = {}

        def early():
            add_core("4", s4)
            held["4"] = sum_phase("4", 2)

        def one():
            add_phase("2", 2, s2)
            held["2"] = sum_phase("2", 1)

        steps = {} if s == 0 else {1: early, 2: one}
        lax.fori_loop(0, blocks[s] + 1, functools.partial(backward, progress=steps), 0)
        if s == 1:
            s2, s4 = held["2"], held["4"]

        def query_back(h, carry, s=s):
            dq = turn_back(OA[h] * 0.0625, CS[s], SN[s])
            raw = QR[h, 256 * s:256 * s + 256, :].astype(F32)
            dv, rowg = norm_back(raw, GV[2:3, 0:256], dq)
            GG[2:3, 0:256] += jnp.sum(rowg, 0, keepdims=True)
            GT[256 * s:256 * s + 256, pl.ds(pl.multiple_of(h * 256, 256), 256)] = dv.astype(BF)
            return carry
        lax.fori_loop(0, 4, query_back, 0)
    for s in range(2):
        HM[256 * s:256 * s + 256, 0:512] = DKV[1 - c if s == 0 else 2 + c].astype(BF)
    dk_cp = send(HM.at[:, pl.ds(0, 512)], DKR, moved("c", 1))

    def do_qkv_grad(n, carry):
        at = pl.ds(pl.multiple_of(n * 512, 512), 512)
        W2[:, :, :, at] = mm(NRMT[...], GT[:, at]).astype(BF).reshape(4, 2, 80, 512)
        return carry
    lax.fori_loop(0, 2, do_qkv_grad, 0)
    s1 = sum_core("1", 0)
    add_phase("3", 2, s3)
    s3 = sum_phase("3", 1)
    add_phase("5", 2, s5)
    s5 = sum_phase("5", 1)
    arrived(dk_cp)
    for s in range(2):
        r = slice(256 * s, 256 * s + 256)
        tot = DKV[blocks[s]] + DKR[r, :].astype(F32)
        dk = turn_back(tot[:, 0:256], CS[s], SN[s])
        dv, rowg = norm_back(KR[r, :], GV[3:4, 0:256], dk)
        GG[3:4, 0:256] += jnp.sum(rowg, 0, keepdims=True)
        GT[r, 1024:1280] = dv.astype(BF)
        GT[r, 1280:1536] = tot[:, 256:512].astype(BF)
    do_qkv_grad(2, 0)
    t1 = sum_core("1", 1)
    add_core("1", s1, 0)
    s1a, s1b = sum_phase("1a", 2, 0), sum_phase("1b", 2, 0)

    def do_dnorm(n, carry):
        at = pl.ds(pl.multiple_of(n * 512, 512), 512)
        part = mm_nt(GT[:, at], w1_cols(n * 512, 512))
        if carry is None:
            ACC[...] = part
        else:
            ACC[...] += part
        return carry
    do_dnorm(0, None)
    add_core("1", t1, 1)
    s1a, s1b = s1a + sum_phase("1a", 2, 1), s1b + sum_phase("1b", 2, 1)
    add_phase("5", 1, s5)
    s5 = sum_phase("5", 0)
    lax.fori_loop(1, 3, do_dnorm, 0)
    add_phase("2", 1, s2)
    s2 = sum_phase("2", 0)
    add_phase("3", 1, s3)
    s3 = sum_phase("3", 0)
    all_gone(lo_sent)
    gxv = LO.reshape(T, D)

    def do_x(r):
        dv, rowg = norm_back(xv[r, :].astype(F32), GV[0:1, :], ACC[r, :])
        GG[0:1, :] += jnp.sum(rowg, 0, keepdims=True)
        gxv[r, :] = (HID[r, :] + dv).astype(BF)
    rows(128, do_x)
    gx_in = unshard(LO, o_gx)

    near = [dict(me, c=(c + dc) % 2, y=(y + dy) % 4) for dc in (0, 1) for dy in range(4) if dc + dy > 0]
    gs = post([(None, GG, GGR.at[i], co) for i, co in enumerate(near)], [(None, GGR.at[pl.ds(0, 7)])])

    def gain_step(axis, base, tot):
        GGR[base + 3] = tot
        return post(
            [(None, GGR.at[base + 3], GGR.at[base + k - 1], moved(axis, k)) for k in (1, 2, 3)],
            [(None, GGR.at[pl.ds(base, 3)])],
        )

    def gain_sum(lo, hi, tot):
        for k in range(lo, hi):
            tot = tot + GGR[k]
        return tot

    def into(k):
        def out(v):
            mf[k] = v.reshape(80, 128)
        return out

    def out_4(v):
        c4f[...] = v.reshape(16, 384)

    def out_down(v):
        MISC[0:16, :] = v.reshape(16, 640)

    add_phase("4", 2, s4)
    s4 = sum_phase("4", 1)
    add_phase("1b", 2, s1b)
    s1b = sum_phase("1b", 1)
    add_phase("1a", 2, s1a)
    s1a = sum_phase("1a", 1)
    arrived(gs)
    tot = gain_sum(0, 7, GG[...])
    gs = gain_step("z", 7, tot)
    add_phase("4", 1, s4)
    s4 = sum_phase("4", 0)
    add_phase("5", 0, s5, out_down)
    add_phase("2", 0, s2, into(1))
    add_phase("3", 0, s3, into(2))
    for e in range(16):
        for k in (1, 2):
            F2[e, 5 * k:5 * k + 5, :] = mf[k, 5 * e:5 * e + 5, :]
    add_phase("1b", 1, s1b)
    add_phase("1a", 1, s1a)
    s1 = sum_phase("1", 0)
    arrived(gs)
    tot = gain_sum(7, 10, tot)
    gs = gain_step("x", 11, tot)
    add_phase("4", 0, s4, out_4)
    pair = send(c4f.at[pl.ds(pl.multiple_of(8 * (1 - y % 2), 8), 8), :], R4, near_y())
    add_phase("1", 0, s1, into(0))
    for e in range(16):
        F2[e, 0:5, :] = mf[0, 5 * e:5 * e + 5, :]
    earlier = list(sent)
    sent.clear()
    home = post(
        [(None, F2.at[(j // 4) % 2 * 8 + j // 8 * 4 + j % 4], o_cols.at[gi], member(j)) for j in others],
        [(None, o_cols.at[pl.ds(0, 15)])],
    )
    keep_cols = pltpu.make_async_copy(F2.at[ge], o_cols.at[gi], ls)
    keep_cols.start()
    MISC[24:32, :] = jnp.zeros((8, D), F32)
    arrived(gs)
    tot = gain_sum(11, 14, tot)
    shard = f * 4 + y
    for k, (_, per, width) in enumerate(GAINS):
        line = tot[k:k + 1, 0:width]
        col = iota((1, width), 1)
        for r in range(per):
            MISC[24 + k:25 + k, r:r + 1] = jnp.sum(jnp.where(col == per * shard + r, line, 0.0), 1, keepdims=True)
    arrived(pair)
    own = c4f[pl.ds(pl.multiple_of(8 * (y % 2), 8), 8), :]
    left = y % 2 == 0
    MISC[16:24, 0:384] = jnp.where(left, own, R4[...])
    MISC[16:24, 384:640] = jnp.where(left, R4[...], own)[:, 0:256]
    keep_cols.wait()
    keep_rows = pltpu.make_async_copy(MISC, o_rows, ls)
    keep_rows.start()
    all_gone(earlier)
    keep_rows.wait()
    arrived(gx_in + lo_in + home)
    all_gone(sent)


def finish(lay, gx, cols, rows, o_layer, o_gx, o_q, o_k, o_v, o_o, o_gate, o_up, o_down, o0, o1, o2, o3, o4, o5):
    o_layer[...] = lay[...]
    for j in range(16):
        at = slice(128 * j, 128 * j + 128)
        v = cols[j]
        if j < 8:
            o_q[:, at] = v[0:5]
        elif j < 10:
            o_k[:, 128 * (j - 8):128 * (j - 7)] = v[0:5]
        elif j < 12:
            o_v[:, 128 * (j - 10):128 * (j - 9)] = v[0:5]
        o_gate[:, at] = v[5:10]
        o_up[:, at] = v[10:15]
    o_down[...] = rows[0:16, :]
    o_o[...] = rows[16:24, :]
    for k, ref in enumerate((o0, o1, o2, o3, o4, o5)):
        ref[...] = rows[24 + k:25 + k, 0:GAINS[k][1]]
    for m in range(2):
        o_gx[m] = gx[m].astype(F32)


def scratch():
    def v(*shape, dtype=F32):
        return pltpu.VMEM(shape, dtype)

    def b(*shape):
        return pltpu.VMEM(shape, BF)

    cols = (4, 2, 80, 2048)
    out = [
        b(*cols), b(*cols), b(*cols), b(4, 4, 2, 32, 768), b(4, 4, 2, 64, 640), b(4, 2, 16, 128),
        v(16, 16, 128), b(16, 16, 128), b(16, 16, 128), v(4, 80, 128), b(2, 16, 384), b(16, 384),
        v(2, 8, 128, dtype=I32),
        b(2, 256, D), b(2, 256, D), b(T, D), b(D, T), b(D, T), b(1024, T),
        v(2, 256, 128), v(2, 256, 128),
        v(2, 256, 1, dtype=I32), v(4, 1, 256, dtype=I32), v(8, D),
        b(4, T, 256), b(2, 4, 256, 256), v(T, 256), b(4, 256, 512), b(T, 1024),
        v(2, 256, 4), v(4, 256, 256), v(4, 256, 1),
        b(T, D), v(T, D), b(T, D), b(T, 2048), b(T, 2048), b(T, 2048), v(T, D), b(T, D),
        b(2, 256, D),
        b(2, 4, 256, 256), v(2, 256, 4), v(4, 256, 512), b(T, 512),
        b(*cols), b(*cols), b(4, 4, 2, 32, 768), b(4, 4, 2, 64, 640),
        b(4, 2, 80, 1024), b(4, 2, 80, 1024), b(4, 2, 80, 1024), b(4, 4, 1, 32, 768), b(4, 4, 1, 64, 640),
        b(3, 1, 2, 48, 1024), b(3, 4, 1, 32, 512), b(3, 1, 2, 80, 1024), b(3, 4, 1, 80, 512),
        b(3, 4, 4, 1, 16, 384), b(3, 4, 4, 1, 16, 640),
        b(3, 1, 1, 48, 512), b(3, 1, 1, 32, 512), b(3, 1, 1, 80, 512), b(3, 1, 1, 80, 512),
        b(3, 1, 4, 1, 16, 384), b(3, 4, 1, 1, 16, 640),
        b(3, 1, 1, 80, 128), b(3, 1, 1, 80, 128), b(3, 1, 1, 80, 128), b(3, 1, 1, 1, 16, 384), b(3, 1, 1, 1, 16, 640),
        v(8, D), v(15, 8, D), v(16, 16, 128), v(16, 384), v(8, 384), v(32, D),
        pltpu.SemaphoreType.DMA((N_SEM,)), pltpu.SemaphoreType.DMA((N_SEM,)), pltpu.SemaphoreType.DMA,
    ]
    return out


def on_device(tokens_in, cotangent, doc_lengths, w_query, w_key, w_value, w_out, gain_attn_in, gain_attn_out,
              gain_query, gain_key, w_gate, w_up, w_down, gain_ffn_in, gain_ffn_out):
    gains = [g.reshape(1, -1) for g in (gain_attn_in, gain_attn_out, gain_query, gain_key, gain_ffn_in, gain_ffn_out)]
    vm = pl.BlockSpec(memory_space=pltpu.VMEM)
    hbm = pl.BlockSpec(memory_space=pl.ANY)

    def s(*shape, dtype=F32):
        return jax.ShapeDtypeStruct(shape, dtype)

    parts = pl.pallas_call(
        kernel,
        out_shape=(s(2, 256, D, dtype=BF), s(2, 256, D, dtype=BF), s(16, 16, 128), s(32, D)),
        in_specs=[hbm, hbm] + [vm] * 14,
        out_specs=(hbm,) * 4,
        scratch_shapes=scratch(),
        compiler_params=pltpu.CompilerParams(
            collective_id=0, has_side_effects=True, vmem_limit_bytes=64 * 1024 * 1024 - 65536
        ),
        name="block",
    )(tokens_in, cotangent, doc_lengths, *gains, w_query, w_key, w_value, w_out, w_gate, w_up, w_down)
    outs = pl.pallas_call(
        finish,
        out_shape=(
            s(2, 256, D, dtype=BF), s(2, 256, D), s(5, 1024), s(5, 256), s(5, 256), s(8, D), s(5, 2048), s(5, 2048),
            s(16, D), s(1, 5), s(1, 5), s(1, 2), s(1, 2), s(1, 5), s(1, 5),
        ),
        in_specs=[vm] * 4,
        out_specs=(vm,) * 15,
        name="finish",
    )(*parts)
    (layer_out, grad_x, gq, gk, gv, go, ggate, gup, gdown, g0, g1, g2, g3, g4, g5) = outs
    return (
        layer_out, grad_x, gq, gk, gv, go, g0.reshape(-1), g1.reshape(-1), g2.reshape(-1), g3.reshape(-1),
        ggate, gup, gdown, g4.reshape(-1), g5.reshape(-1),
    )


def solution(mesh):
    both = ("fsdp", "dp")
    row, gain = P(both, None), P(both)
    tok = P(None, both, None)
    return jax.shard_map(
        on_device,
        mesh=mesh,
        in_specs=(tok, tok, P("fsdp", None, None), row, row, row, row, gain, gain, gain, gain, row, row, row, gain, gain),
        out_specs=(tok, tok, row, row, row, row, gain, gain, gain, gain, row, row, row, gain, gain),
        check_vma=False,
    )
```
